256 devices in a mesh: rep: 4 (over x_lo, core), ctx: 64 (over z, y, x_hi).
Axes of the slice: x: 4 (x_hi: 2, x_lo: 2; x = x_hi * 2 + x_lo), y: 4, z: 8, core: 2. Of those that a mesh axis runs over, the one named last changes fastest.
Arguments:
- grad_out: bfloat16 [4, 2048, 8192], P('rep', None, 'ctx'), may hold values from -6 to 6
- gate: bfloat16 [4, 2048, 8192], P('rep', None, 'ctx'), may hold values from -6 to 6
- values: bfloat16 [4, 2048, 8192], P('rep', None, 'ctx'), may hold values from -6 to 6
- filters: float32 [2048, 8192], P('ctx'), may hold values from -0.0625 to 0.0625
- skip: float32 [2048], P('ctx'), may hold values from 0.5 to 1.5
Outputs:
- d_values: bfloat16 [4, 2048, 8192], P('rep', None, 'ctx')
- d_gate: bfloat16 [4, 2048, 8192], P('rep', None, 'ctx')
- d_filter: float32 [2048, 8192], P('ctx')
The draws below stay inside these ranges and needn't reach their ends.
All inputs are finite; a program needn't handle non-finite values.
Results may differ from the reference program's by a relative error of at most 0.005.
Values may be sent and summed in bfloat16 or wider, within the bound.
A program may use at most 64 MiB of HBM per device.

```python
import math
import jax
import jax.numpy as jnp
from jax import lax

CHANNELS = 2048
SEQ = 8192
REPS = 4
N_REP = 4


def level_of(stream_key, shape, cuts, smallest, high):
    loudness = 1.0
    for dim, blocks in cuts:
        steps = jax.random.uniform(jax.random.fold_in(jax.random.fold_in(stream_key, 6), dim), (blocks,), jnp.float32, smallest / len(cuts), high / len(cuts))
        loudness = loudness * jnp.repeat(jnp.exp(steps), shape[dim] // blocks).reshape((-1,) + (1,) * (len(shape) - 1 - dim))
    return loudness


def noise(stream_key, shape, deviation, bound, shards=(), held_as=jnp.bfloat16):
    array = deviation * jax.random.normal(stream_key, shape, jnp.float32)
    if shards:
        array = array * level_of(stream_key, shape, shards, -0.22, 0.18)
    return jnp.clip(array, -bound, bound).astype(held_as)


def setup_inputs(seed: int = 0) -> dict:
    key_of = jax.random.split(jax.random.key(seed), 6)
    grad_out = noise(key_of[0], (REPS, CHANNELS, SEQ), 1.0, 6.0, ((0, 4), (2, 64)))
    gate = noise(key_of[1], (REPS, CHANNELS, SEQ), 1.0, 6.0, ((0, 4), (2, 64)))
    values = noise(key_of[2], (REPS, CHANNELS, SEQ), 1.0, 6.0, ((0, 4), (2, 64)))
    filters = noise(key_of[3], (CHANNELS, SEQ), SEQ ** -0.5, 0.0625, ((0, 64),), jnp.float32)
    skip = jnp.clip(0.5 + 1.0 * jax.random.uniform(key_of[4], (CHANNELS,), jnp.float32) ** level_of(key_of[4], (CHANNELS,), ((0, 64),), -0.2, 0.2), 0.5, 1.5)
    return dict(grad_out=grad_out, gate=gate, values=values, filters=filters, skip=skip)


def reference(grad_out, gate, values, filters, skip):
    length = 2 * SEQ
    filter_spec = jnp.fft.rfft(filters, n=length, axis=-1)
    skip_col = skip[:, None]

    def one_sequence(items):
        grad_seq, gate_seq, value_seq = items
        d_conv = (grad_seq.astype(jnp.float32) * gate_seq.astype(jnp.float32)).astype(jnp.bfloat16)
        d_conv = lax.optimization_barrier(d_conv)
        value_f = value_seq.astype(jnp.float32)
        conv_f = d_conv.astype(jnp.float32)
        value_spec = jnp.fft.rfft(value_f, n=length, axis=-1)
        conv_spec = jnp.fft.rfft(conv_f, n=length, axis=-1)
        forward_conv = jnp.fft.irfft(filter_spec * value_spec, n=length, axis=-1)[:, :SEQ]
        back_conv = jnp.fft.irfft(jnp.conj(filter_spec) * conv_spec, n=length, axis=-1)[:, :SEQ]
        mixed = (forward_conv + skip_col * value_f).astype(jnp.bfloat16)
        mixed = lax.optimization_barrier(mixed)
        d_gate = (grad_seq.astype(jnp.float32) * mixed.astype(jnp.float32)).astype(jnp.bfloat16)
        d_values = (back_conv + skip_col * conv_f).astype(jnp.bfloat16)
        filter_part = jnp.fft.irfft(conv_spec * jnp.conj(value_spec), n=length, axis=-1)[:, :SEQ]
        return (d_values, d_gate, filter_part.astype(filters.dtype))
    d_values, d_gate, filter_parts = lax.map(one_sequence, (grad_out, gate, values))
    d_filter = lax.optimization_barrier(jnp.sum(filter_parts, axis=0)) * (1.0 / math.sqrt(N_REP * SEQ))
    return (d_values, d_gate, d_filter)
```

```python
import functools
import math

import jax
import jax.numpy as jnp
import ml_dtypes
import numpy as np
from jax import lax
from jax.experimental import pallas as pl
from jax.experimental.pallas import tpu as pltpu
from jax.sharding import PartitionSpec as P

F32 = jnp.float32
BF16 = jnp.bfloat16


def split_np(table):
    high = table.astype(ml_dtypes.bfloat16)
    low = (table - high.astype(np.float64)).astype(ml_dtypes.bfloat16)
    return high, low


@functools.lru_cache(None)
def tables(chunks, width):
    total = chunks * width
    n = np.arange(chunks)
    q = np.arange(width)
    outer = 2 * np.pi * np.outer(n + 0.25, n) / chunks
    turn = 2 * np.pi * np.outer(n + 0.25, q) / total
    inner = 2 * np.pi * (np.outer(q, q) % width) / width
    first = np.concatenate([np.cos(outer), -np.sin(outer)], axis=0)
    first_hi, first_lo = split_np(first)
    fwd_first = np.concatenate([first_hi, first_lo], axis=1)
    filter_first = np.concatenate([first_hi, first_hi, first_lo], axis=1)
    cos, sin = np.cos(inner), np.sin(inner)
    second = np.block([[cos, -sin], [sin, cos]])
    second_hi, second_lo = split_np(second)
    back_hi, back_lo = split_np(second.T)
    last = np.concatenate([np.cos(outer).T, -np.sin(outer).T], axis=1)
    last_hi, last_lo = split_np(last)
    zero = np.zeros_like(last_lo)
    inv_last = np.concatenate(
        [np.concatenate([last_hi, last_hi], axis=1), np.concatenate([last_lo, zero], axis=1)], axis=0
    )
    twist = np.stack([np.cos(turn), np.sin(turn)]).astype(np.float32)
    return fwd_first, filter_first, second_hi, second_lo, back_hi, back_lo, inv_last, twist


def dot(left, right):
    return jnp.dot(left, right, preferred_element_type=F32)


def split(array):
    high = array.astype(BF16)
    low = (array - high.astype(F32)).astype(BF16)
    return high, low


def dot3(left, right_hi, right_lo):
    high, low = split(left)
    return dot(high, right_hi) + (dot(low, right_hi) + dot(high, right_lo))


def pack_kernel(grad_ref, gate_ref, value_ref, out_ref):
    rows, width = grad_ref.shape
    groups = rows // 8
    d_conv = grad_ref[...].astype(F32) * gate_ref[...].astype(F32)
    value = value_ref[...].astype(F32)
    both = jnp.concatenate([value.reshape(groups, 8, width), d_conv.reshape(groups, 8, width)], axis=1)
    out_ref[...] = both.astype(BF16)


def unpack_kernel(back_ref, grad_ref, d_values_ref, d_gate_ref):
    groups, _, width = back_ref.shape
    back = back_ref[...].astype(F32)
    grad = grad_ref[...].astype(F32)
    mixed = back[:, :8].reshape(groups * 8, width)
    d_values_ref[...] = back[:, 8:].reshape(groups * 8, width).astype(BF16)
    d_gate_ref[...] = (grad * mixed).astype(BF16)


def conv_kernel(
    reps, chunks, width,
    skip_ref, data_ref, filter_ref,
    first_ref, filter_first_ref, second_hi_ref, second_lo_ref, back_hi_ref, back_lo_ref, last_ref, twist_ref,
    out_ref, d_filter_ref,
    rows_in, rows_out, filter_rows, filter_spec, cross, spectra,
):
    here = 8
    mine = lax.axis_index("rep") * here
    scale = 1.0 / (chunks * width)

    def twisted(section):
        cos, sin = twist_ref[0], twist_ref[1]
        real, imag = section[:chunks], section[chunks:]
        return jnp.concatenate([real * cos + imag * sin, imag * cos - real * sin], axis=1)

    def untwisted(section):
        cos, sin = twist_ref[0], twist_ref[1]
        real, imag = section[:, :width], section[:, width:]
        return jnp.concatenate([real * cos - imag * sin, imag * cos + real * sin], axis=0)

    for n in range(chunks):
        filter_rows[n * here:(n + 1) * here, :] = filter_ref[pl.ds(mine, here), n * width:(n + 1) * width]

    @pl.loop(0, here)
    def _(c):
        high, low = split(filter_rows[pl.ds(c, chunks, stride=here), :])
        section = dot(filter_first_ref[...], jnp.concatenate([high, low, high], axis=0))
        filter_spec[c] = dot3(twisted(section), second_hi_ref[...], second_lo_ref[...]) * scale
        cross[c] = jnp.zeros((chunks, 2 * width), F32)

    @pl.loop(0, reps)
    def _(r):
        rows_in[...] = data_ref[:, r].astype(F32).reshape(chunks * 16, width)

        @pl.loop(0, here)
        def _(c):
            value = rows_in[pl.ds(c, chunks, stride=16), :].astype(BF16)
            d_conv = rows_in[pl.ds(c + here, chunks, stride=16), :].astype(BF16)
            pair = jnp.concatenate([value, d_conv], axis=1)
            section = dot(first_ref[...], jnp.concatenate([pair, pair], axis=0))
            spectra[c] = jnp.concatenate([twisted(section[:, :width]), twisted(section[:, width:])], axis=0)

        flat = spectra[...].reshape(here * 2 * chunks, 2 * width)
        spectra[...] = dot3(flat, second_hi_ref[...], second_lo_ref[...]).reshape(spectra.shape)

        @pl.loop(0, here)
        def _(c):
            vr, vi = spectra[c, :chunks, :width], spectra[c, :chunks, width:]
            dr, di = spectra[c, chunks:, :width], spectra[c, chunks:, width:]
            fr, fi = filter_spec[c, :, :width], filter_spec[c, :, width:]
            cross[c, :, :width] += dr * vr + di * vi
            cross[c, :, width:] += di * vr - dr * vi
            spectra[c, :chunks, :width] = fr * vr - fi * vi
            spectra[c, :chunks, width:] = fr * vi + fi * vr
            spectra[c, chunks:, :width] = fr * dr + fi * di
            spectra[c, chunks:, width:] = fr * di - fi * dr

        flat = spectra[...].reshape(here * 2 * chunks, 2 * width)
        spectra[...] = dot3(flat, back_hi_ref[...], back_lo_ref[...]).reshape(spectra.shape)

        @pl.loop(0, here)
        def _(c):
            skip = skip_ref[mine + c]
            both = jnp.concatenate(
                [untwisted(spectra[c, :chunks]), untwisted(spectra[c, chunks:])], axis=1
            )
            high, low = split(both)
            parts = dot(last_ref[...], jnp.concatenate([high, low], axis=0))
            result = parts[:chunks] + parts[chunks:]
            value = rows_in[pl.ds(c, chunks, stride=16), :]
            d_conv = rows_in[pl.ds(c + here, chunks, stride=16), :]
            rows_out[pl.ds(c, chunks, stride=16), :] = result[:, :width] + skip * value
            rows_out[pl.ds(c + here, chunks, stride=16), :] = result[:, width:] + skip * d_conv

        out_ref[:, r] = rows_out[...].reshape(chunks, 16, width).astype(BF16)

    factor = scale / math.sqrt(reps * chunks * width)

    @pl.loop(0, here)
    def _(c):
        both = untwisted(dot3(cross[c] * factor, back_hi_ref[...], back_lo_ref[...]))
        high, low = split(both)
        parts = dot(last_ref[...], jnp.concatenate([high, low], axis=0))
        filter_rows[pl.ds(c, chunks, stride=here), :] = parts[:chunks] + parts[chunks:]

    for n in range(chunks):
        d_filter_ref[:, n * width:(n + 1) * width] = filter_rows[n * here:(n + 1) * here, :]


def on_device(grad_out, gate, values, filters, skip):
    reps = lax.axis_size("rep")
    chunks = lax.axis_size("ctx")
    channels, width = values.shape[1:]
    groups = channels // 8
    vmem = pl.BlockSpec(memory_space=pltpu.VMEM)
    smem = pl.BlockSpec(memory_space=pltpu.SMEM)
    params = pltpu.CompilerParams(vmem_limit_bytes=56 * 1024 * 1024)
    grad_out, gate, values = grad_out[0], gate[0], values[0]
    packed = pl.pallas_call(
        pack_kernel,
        out_shape=jax.ShapeDtypeStruct((groups, 16, width), BF16),
        in_specs=[vmem] * 3,
        out_specs=vmem,
        compiler_params=params,
        name="pack",
    )(grad_out, gate, values)
    rows = lax.all_to_all(packed, ("ctx", "rep"), split_axis=0, concat_axis=0, tiled=True)
    rows = rows.reshape(chunks, reps, 16, width)
    consts = [jnp.asarray(t) for t in tables(chunks, width)]
    results, d_filter = pl.pallas_call(
        functools.partial(conv_kernel, reps, chunks, width),
        out_shape=[
            jax.ShapeDtypeStruct((chunks, reps, 16, width), BF16),
            jax.ShapeDtypeStruct((8, chunks * width), F32),
        ],
        in_specs=[smem] + [vmem] * (2 + len(consts)),
        out_specs=[vmem, vmem],
        scratch_shapes=[
            pltpu.VMEM((chunks * 16, width), F32),
            pltpu.VMEM((chunks * 16, width), F32),
            pltpu.VMEM((chunks * 8, width), F32),
            pltpu.VMEM((8, chunks, 2 * width), F32),
            pltpu.VMEM((8, chunks, 2 * width), F32),
            pltpu.VMEM((8, 2 * chunks, 2 * width), F32),
        ],
        compiler_params=params,
        name="conv",
    )(skip, rows, filters, *consts)
    results = results.reshape(groups, 16, width)
    back = lax.all_to_all(results, ("ctx", "rep"), split_axis=0, concat_axis=0, tiled=True)
    d_filter = lax.all_gather(d_filter, "rep", axis=0, tiled=True)
    d_values, d_gate = pl.pallas_call(
        unpack_kernel,
        out_shape=[jax.ShapeDtypeStruct((channels, width), BF16)] * 2,
        in_specs=[vmem] * 2,
        out_specs=[vmem] * 2,
        compiler_params=params,
        name="unpack",
    )(back, grad_out)
    return d_values[None], d_gate[None], d_filter


def solution(mesh):
    placed = (
        P("rep", None, "ctx"),
        P("rep", None, "ctx"),
        P("rep", None, "ctx"),
        P("ctx", None),
        P("ctx"),
    )
    return jax.shard_map(
        on_device,
        mesh=mesh,
        in_specs=placed,
        out_specs=(P("rep", None, "ctx"), P("rep", None, "ctx"), P("ctx", None)),
        check_vma=False,
    )
```

```python
import functools
import math

import jax
import jax.numpy as jnp
import ml_dtypes
import numpy as np
from jax import lax
from jax.experimental import pallas as pl
from jax.experimental.pallas import tpu as pltpu
from jax.sharding import PartitionSpec as P

MESH = pl.DeviceIdType.MESH
F32 = jnp.float32
BF16 = jnp.bfloat16


def split_np(table):
    high = table.astype(ml_dtypes.bfloat16)
    low = (table - high.astype(np.float64)).astype(ml_dtypes.bfloat16)
    return high, low


@functools.lru_cache(None)
def tables(chunks, width):
    total = chunks * width
    n = np.arange(chunks)
    q = np.arange(width)
    outer = 2 * np.pi * np.outer(n + 0.25, n) / chunks
    turn = 2 * np.pi * np.outer(n + 0.25, q) / total
    inner = 2 * np.pi * (np.outer(q, q) % width) / width
    first = np.concatenate([np.cos(outer), -np.sin(outer)], axis=0)
    first_hi, first_lo = split_np(first)
    fwd_first = np.concatenate([first_hi, first_lo], axis=1)
    filter_first = np.concatenate([first_hi, first_hi, first_lo], axis=1)
    cos, sin = np.cos(inner), np.sin(inner)
    second = np.block([[cos, -sin], [sin, cos]])
    second_hi, second_lo = split_np(second)
    back_hi, back_lo = split_np(second.T)
    last = np.concatenate([np.cos(outer).T, -np.sin(outer).T], axis=1)
    last_hi, last_lo = split_np(last)
    zero = np.zeros_like(last_lo)
    inv_last = np.concatenate(
        [np.concatenate([last_hi, last_hi], axis=1), np.concatenate([last_lo, zero], axis=1)], axis=0
    )
    twist = np.stack([np.cos(turn), np.sin(turn)]).astype(np.float32)
    return fwd_first, filter_first, second_hi, second_lo, back_hi, back_lo, inv_last, twist


def dot(left, right):
    return jnp.dot(left, right, preferred_element_type=F32)


def split(array):
    high = array.astype(BF16)
    low = (array - high.astype(F32)).astype(BF16)
    return high, low


def dot3(left, right_hi, right_lo):
    high, low = split(left)
    return dot(high, right_hi) + (dot(low, right_hi) + dot(high, right_lo))


def whole_kernel(
    reps, chunks, width, grid,
    skip_ref, grad_ref, gate_ref, value_ref, filter_ref,
    first_ref, filter_first_ref, second_hi_ref, second_lo_ref, back_hi_ref, back_lo_ref, last_ref, twist_ref,
    d_values_ref, d_gate_ref, d_filter_ref,
    send, recv, result_out, back, rows_in, rows_out, filter_rows, filter_spec, cross, spectra, note_out, note_in,
    send_sem, recv_sem, back_send_sem, back_sem, filter_send_sem, filter_sem, note_send_sem, note_sem,
):
    here = 8
    nz, ny, nx = grid
    rep = lax.axis_index("rep")
    ctx = lax.axis_index("ctx")
    z, y, x = ctx // (ny * nx), (ctx // nx) % ny, ctx % nx
    mine = rep * here
    scale = 1.0 / (chunks * width)

    def place(zz, yy, xx):
        return (zz % nz) * (ny * nx) + (yy % ny) * nx + xx % nx

    def along_row(step):
        return rep, place(z + step // nx, y, x + step % nx)

    def along_column(step):
        return (rep + step // ny) % reps, place(z, y + step % ny, x)

    def swing(step, size):
        return (step + 1) // 2 * (2 * (step % 2) - 1) + size

    def partner(step):
        rest = step // nz
        return place(z + swing(step % nz, nz), y + swing(rest // nx, ny), x + rest % nx)

    def peer(phase):
        base = (rep + phase // 2 * 2) % reps
        return base + phase % 2 * (1 - base % 2 * 2)

    def twisted(section):
        cos, sin = twist_ref[0], twist_ref[1]
        real, imag = section[:chunks], section[chunks:]
        return jnp.concatenate([real * cos + imag * sin, imag * cos - real * sin], axis=1)

    def untwisted(section):
        cos, sin = twist_ref[0], twist_ref[1]
        real, imag = section[:, :width], section[:, width:]
        return jnp.concatenate([real * cos - imag * sin, imag * cos + real * sin], axis=0)

    barrier = pltpu.get_barrier_semaphore()

    @pl.loop(1, nz * nx)
    def _(step):
        pl.semaphore_signal(barrier, 1, device_id=along_row(step), device_id_type=MESH)

    @pl.loop(1, reps * ny)
    def _(step):
        pl.semaphore_signal(barrier, 1, device_id=along_column(step), device_id_type=MESH)

    @pl.loop(0, chunks)
    def _(j):
        value = value_ref[j].astype(F32)
        d_conv = grad_ref[j].astype(F32) * gate_ref[j].astype(F32)
        both = jnp.concatenate([value.reshape(reps, here, width), d_conv.reshape(reps, here, width)], axis=1)
        send[j] = both.astype(BF16)

    note_out[...] = jnp.zeros_like(note_out)
    recv[0, ctx] = send[ctx, rep]
    pl.semaphore_wait(barrier, nz * nx + reps * ny - 2)

    def note(step):
        return pltpu.make_async_remote_copy(
            src_ref=note_out, dst_ref=note_in.at[rep * ny + y],
            send_sem=note_send_sem, recv_sem=note_sem, device_id=along_column(step), device_id_type=MESH,
        )

    @pl.loop(1, reps * ny)
    def _(step):
        note(step).start()

    for n in range(chunks):
        filter_rows[n * here:(n + 1) * here, :] = filter_ref[pl.ds(mine, here), n * width:(n + 1) * width]

    count = reps * ny - 1
    pltpu.make_async_copy(note_in.at[pl.ds(0, count)], note_in.at[pl.ds(0, count)], note_sem).wait()
    pltpu.make_async_copy(note_in.at[pl.ds(0, count)], note_in.at[pl.ds(0, count)], note_send_sem).wait()

    @pl.loop(1, reps * chunks)
    def _(step):
        phase = step // chunks
        i, j = peer(phase), partner(step % chunks)
        pltpu.make_async_remote_copy(
            src_ref=send.at[j, i], dst_ref=recv.at[phase, ctx],
            send_sem=send_sem, recv_sem=recv_sem.at[phase], device_id=(i, j), device_id_type=MESH,
        ).start()

    @pl.loop(0, here)
    def _(c):
        high, low = split(filter_rows[pl.ds(c, chunks, stride=here), :])
        section = dot(filter_first_ref[...], jnp.concatenate([high, low, high], axis=0))
        filter_spec[c] = dot3(twisted(section), second_hi_ref[...], second_lo_ref[...]) * scale
        cross[c] = jnp.zeros((chunks, 2 * width), F32)

    def convolve(phase):
        rows_in[...] = recv[phase].astype(F32).reshape(chunks * 16, width)

        @pl.loop(0, here)
        def _(c):
            value = rows_in[pl.ds(c, chunks, stride=16), :].astype(BF16)
            d_conv = rows_in[pl.ds(c + here, chunks, stride=16), :].astype(BF16)
            pair = jnp.concatenate([value, d_conv], axis=1)
            section = dot(first_ref[...], jnp.concatenate([pair, pair], axis=0))
            spectra[c] = jnp.concatenate([twisted(section[:, :width]), twisted(section[:, width:])], axis=0)

        flat = spectra[...].reshape(here * 2 * chunks, 2 * width)
        spectra[...] = dot3(flat, second_hi_ref[...], second_lo_ref[...]).reshape(spectra.shape)

        @pl.loop(0, here)
        def _(c):
            vr, vi = spectra[c, :chunks, :width], spectra[c, :chunks, width:]
            dr, di = spectra[c, chunks:, :width], spectra[c, chunks:, width:]
            fr, fi = filter_spec[c, :, :width], filter_spec[c, :, width:]
            cross[c, :, :width] += dr * vr + di * vi
            cross[c, :, width:] += di * vr - dr * vi
            spectra[c, :chunks, :width] = fr * vr - fi * vi
            spectra[c, :chunks, width:] = fr * vi + fi * vr
            spectra[c, chunks:, :width] = fr * dr + fi * di
            spectra[c, chunks:, width:] = fr * di - fi * dr

        flat = spectra[...].reshape(here * 2 * chunks, 2 * width)
        spectra[...] = dot3(flat, back_hi_ref[...], back_lo_ref[...]).reshape(spectra.shape)

        @pl.loop(0, here)
        def _(c):
            skip = skip_ref[mine + c]
            both = jnp.concatenate(
                [untwisted(spectra[c, :chunks]), untwisted(spectra[c, chunks:])], axis=1
            )
            high, low = split(both)
            parts = dot(last_ref[...], jnp.concatenate([high, low], axis=0))
            result = parts[:chunks] + parts[chunks:]
            value = rows_in[pl.ds(c, chunks, stride=16), :]
            d_conv = rows_in[pl.ds(c + here, chunks, stride=16), :]
            rows_out[pl.ds(c, chunks, stride=16), :] = result[:, :width] + skip * value
            rows_out[pl.ds(c + here, chunks, stride=16), :] = result[:, width:] + skip * d_conv

        result_out[phase] = rows_out[...].reshape(chunks, 16, width).astype(BF16)

    def send_back(phase, start):
        other = peer(phase)

        @pl.loop(start, chunks)
        def _(step):
            j = partner(step)
            pltpu.make_async_remote_copy(
                src_ref=result_out.at[phase, j], dst_ref=back.at[ctx, rep],
                send_sem=back_send_sem, recv_sem=back_sem.at[phase], device_id=(other, j), device_id_type=MESH,
            ).start()

    for phase in range(reps):
        blocks = chunks - 1 if phase == 0 else chunks
        arrived = recv.at[phase, pl.ds(0, blocks)]
        pltpu.make_async_copy(arrived, arrived, recv_sem.at[phase]).wait()
        convolve(phase)
        if phase == 0:
            back[ctx, rep] = result_out[0, ctx]
        send_back(phase, 1 if phase == 0 else 0)

    factor = scale / math.sqrt(reps * chunks * width)

    @pl.loop(0, here)
    def _(c):
        both = untwisted(dot3(cross[c] * factor, back_hi_ref[...], back_lo_ref[...]))
        high, low = split(both)
        parts = dot(last_ref[...], jnp.concatenate([high, low], axis=0))
        filter_rows[pl.ds(c, chunks, stride=here), :] = parts[:chunks] + parts[chunks:]

    own = pl.ds(pl.multiple_of(mine, here), here)
    for n in range(chunks):
        d_filter_ref[own, n * width:(n + 1) * width] = filter_rows[n * here:(n + 1) * here, :]

    filter_copies = []
    for phase in range(1, reps):
        filter_copies.append(pltpu.make_async_remote_copy(
            src_ref=d_filter_ref.at[own], dst_ref=d_filter_ref.at[own],
            send_sem=filter_send_sem.at[phase], recv_sem=filter_sem.at[phase],
            device_id=(peer(phase), ctx), device_id_type=MESH,
        ))
        filter_copies[-1].start()

    for half in range(reps // 2):
        for phase in (2 * half, 2 * half + 1):
            blocks = chunks - 1 if phase == 0 else chunks
            arrived = recv.at[phase, pl.ds(0, blocks)]
            pltpu.make_async_copy(arrived, arrived, back_sem.at[phase]).wait()
        side = (rep // 2 + half) % 2
        rows = pl.ds(pl.multiple_of(side * 16, 16), 16)

        @pl.loop(0, chunks)
        def _(k):
            block = back[k, pl.ds(side * 2, 2)].astype(F32)
            mixed = block[:, :here].reshape(16, width)
            d_values_ref[k, rows] = block[:, here:].reshape(16, width).astype(BF16)
            d_gate_ref[k, rows] = (grad_ref[k, rows].astype(F32) * mixed).astype(BF16)

    for copy in filter_copies:
        copy.wait()
    sent = send.at[pl.ds(0, chunks - 1)]
    rest = send.at[chunks - 1, pl.ds(0, reps - 1)]
    for sem in (send_sem, back_send_sem):
        pltpu.make_async_copy(sent, sent, sem).wait()
        pltpu.make_async_copy(rest, rest, sem).wait()


def on_device(grid, grad_out, gate, values, filters, skip):
    reps = lax.axis_size("rep")
    chunks = lax.axis_size("ctx")
    channels, width = values.shape[1:]
    vmem = pl.BlockSpec(memory_space=pltpu.VMEM)
    smem = pl.BlockSpec(memory_space=pltpu.SMEM)
    grad_out, gate, values = (a.reshape(chunks, channels // chunks, width) for a in (grad_out, gate, values))
    consts = [jnp.asarray(t) for t in tables(chunks, width)]
    rows = chunks * 16
    blocks = (reps, chunks, 16, width)
    blocks_back = (chunks, reps, 16, width)
    d_values, d_gate, d_filter = pl.pallas_call(
        functools.partial(whole_kernel, reps, chunks, width, grid),
        out_shape=[
            jax.ShapeDtypeStruct(values.shape, BF16),
            jax.ShapeDtypeStruct(values.shape, BF16),
            jax.ShapeDtypeStruct(filters.shape, F32),
        ],
        in_specs=[smem] + [vmem] * (4 + len(consts)),
        out_specs=[vmem] * 3,
        scratch_shapes=[
            pltpu.VMEM(blocks_back, BF16),
            pltpu.VMEM(blocks, BF16),
            pltpu.VMEM(blocks, BF16),
            pltpu.VMEM(blocks_back, BF16),
            pltpu.VMEM((rows, width), F32),
            pltpu.VMEM((rows, width), F32),
            pltpu.VMEM((chunks * 8, width), F32),
            pltpu.VMEM((8, chunks, 2 * width), F32),
            pltpu.VMEM((8, chunks, 2 * width), F32),
            pltpu.VMEM((8, 2 * chunks, 2 * width), F32),
            pltpu.VMEM((8, width), F32),
            pltpu.VMEM((reps * grid[1], 8, width), F32),
            pltpu.SemaphoreType.DMA,
            pltpu.SemaphoreType.DMA((reps,)),
            pltpu.SemaphoreType.DMA,
            pltpu.SemaphoreType.DMA((reps,)),
            pltpu.SemaphoreType.DMA((reps,)),
            pltpu.SemaphoreType.DMA((reps,)),
            pltpu.SemaphoreType.DMA,
            pltpu.SemaphoreType.DMA,
        ],
        compiler_params=pltpu.CompilerParams(
            vmem_limit_bytes=56 * 1024 * 1024, collective_id=0, has_side_effects=True
        ),
        name="whole",
    )(skip, grad_out, gate, values, filters, *consts)
    return d_values.reshape(1, channels, width), d_gate.reshape(1, channels, width), d_filter


def solution(mesh):
    placed = (
        P("rep", None, "ctx"),
        P("rep", None, "ctx"),
        P("rep", None, "ctx"),
        P("ctx", None),
        P("ctx"),
    )
    grid = (mesh.shape["ctx"] // 8, 4, 2)
    return jax.shard_map(
        functools.partial(on_device, grid),
        mesh=mesh,
        in_specs=placed,
        out_specs=(P("rep", None, "ctx"), P("rep", None, "ctx"), P("ctx", None)),
        check_vma=False,
    )
```

```python
import functools
import math

import jax
import jax.numpy as jnp
import ml_dtypes
import numpy as np
from jax import lax
from jax.experimental import pallas as pl
from jax.experimental.pallas import tpu as pltpu
from jax.sharding import PartitionSpec as P

MESH = pl.DeviceIdType.MESH
F32 = jnp.float32
BF16 = jnp.bfloat16


def split_np(table):
    high = table.astype(ml_dtypes.bfloat16)
    low = (table - high.astype(np.float64)).astype(ml_dtypes.bfloat16)
    return high, low


@functools.lru_cache(None)
def tables(chunks, width):
    total = chunks * width
    n = np.arange(chunks)
    q = np.arange(width)
    outer = 2 * np.pi * np.outer(n + 0.25, n) / chunks
    turn = 2 * np.pi * np.outer(n + 0.25, q) / total
    inner = 2 * np.pi * (np.outer(q, q) % width) / width
    first = np.concatenate([np.cos(outer), -np.sin(outer)], axis=0)
    first_hi, first_lo = split_np(first)
    fwd_first = np.concatenate([first_hi, first_lo], axis=1)
    filter_first = np.concatenate([first_hi, first_hi, first_lo], axis=1)
    cos, sin = np.cos(inner), np.sin(inner)
    second = np.block([[cos, -sin], [sin, cos]])
    second_hi, second_lo = split_np(second)
    back_hi, back_lo = split_np(second.T)
    last = np.concatenate([np.cos(outer).T, -np.sin(outer).T], axis=1)
    last_hi, last_lo = split_np(last)
    zero = np.zeros_like(last_lo)
    inv_last = np.concatenate(
        [np.concatenate([last_hi, last_hi], axis=1), np.concatenate([last_lo, zero], axis=1)], axis=0
    )
    twist = np.stack([np.cos(turn), np.sin(turn)]).astype(np.float32)
    return fwd_first, filter_first, second_hi, second_lo, back_hi, back_lo, inv_last, twist


def dot(left, right):
    return jnp.dot(left, right, preferred_element_type=F32)


def split(array):
    high = array.astype(BF16)
    low = (array - high.astype(F32)).astype(BF16)
    return high, low


def dot3(left, right_hi, right_lo):
    high, low = split(left)
    return dot(high, right_hi) + (dot(low, right_hi) + dot(high, right_lo))


def whole_kernel(
    reps, chunks, width, grid,
    skip_hbm, grad_hbm, gate_hbm, value_hbm, filter_hbm,
    first_hbm, filter_first_hbm, second_hi_hbm, second_lo_hbm, back_hi_hbm, back_lo_hbm, last_hbm, twist_hbm,
    d_values_hbm, d_gate_hbm, d_filter_hbm,
    skip_ref, grad_ref, gate_ref, value_ref, filter_ref,
    first_ref, filter_first_ref, second_hi_ref, second_lo_ref, back_hi_ref, back_lo_ref, last_ref, twist_ref,
    d_values_ref, d_gate_ref, d_filter_ref,
    send, recv, result_out, back, rows_in, rows_out, filter_rows, filter_spec, cross, spectra, note_out, note_in,
    in_sem, out_sem,
    send_sem, recv_sem, back_send_sem, back_sem, filter_send_sem, filter_sem, note_send_sem, note_sem,
):
    here = 8
    nz, ny, nx = grid
    rep = lax.axis_index("rep")
    ctx = lax.axis_index("ctx")
    z, y, x = ctx // (ny * nx), (ctx // nx) % ny, ctx % nx
    mine = rep * here
    scale = 1.0 / (chunks * width)

    def place(zz, yy, xx):
        return (zz % nz) * (ny * nx) + (yy % ny) * nx + xx % nx

    def along_row(step):
        return rep, place(z + step // nx, y, x + step % nx)

    def along_column(step):
        return (rep + step // ny) % reps, place(z, y + step % ny, x)

    def swing(step, size):
        return (step + 1) // 2 * (2 * (step % 2) - 1) + size

    def partner(step):
        rest = step // nz
        return place(z + swing(step % nz, nz), y + swing(rest // nx, ny), x + rest % nx)

    def peer(phase):
        base = (rep + phase // 2 * 2) % reps
        return base + phase % 2 * (1 - base % 2 * 2)

    def twisted(section):
        cos, sin = twist_ref[0], twist_ref[1]
        real, imag = section[:chunks], section[chunks:]
        return jnp.concatenate([real * cos + imag * sin, imag * cos - real * sin], axis=1)

    def untwisted(section):
        cos, sin = twist_ref[0], twist_ref[1]
        real, imag = section[:, :width], section[:, width:]
        return jnp.concatenate([real * cos - imag * sin, imag * cos + real * sin], axis=0)

    own = pl.ds(pl.multiple_of(mine, here), here)
    loads = [
        pltpu.make_async_copy(src, dst, in_sem.at[n])
        for n, (src, dst) in enumerate((
            (grad_hbm, grad_ref), (gate_hbm, gate_ref), (value_hbm, value_ref),
            (filter_hbm.at[own], filter_ref), (filter_first_hbm, filter_first_ref), (twist_hbm, twist_ref),
            (second_hi_hbm, second_hi_ref), (second_lo_hbm, second_lo_ref), (first_hbm, first_ref),
            (back_hi_hbm, back_hi_ref), (back_lo_hbm, back_lo_ref), (last_hbm, last_ref), (skip_hbm, skip_ref),
        ))
    ]
    for load in loads:
        load.start()

    barrier = pltpu.get_barrier_semaphore()

    @pl.loop(1, nz * nx)
    def _(step):
        pl.semaphore_signal(barrier, 1, device_id=along_row(step), device_id_type=MESH)

    @pl.loop(1, reps * ny)
    def _(step):
        pl.semaphore_signal(barrier, 1, device_id=along_column(step), device_id_type=MESH)

    for load in loads[:3]:
        load.wait()

    @pl.loop(0, chunks)
    def _(j):
        value = value_ref[j].astype(F32)
        d_conv = grad_ref[j].astype(F32) * gate_ref[j].astype(F32)
        both = jnp.concatenate([value.reshape(reps, here, width), d_conv.reshape(reps, here, width)], axis=1)
        send[j] = both.astype(BF16)

    note_out[...] = jnp.zeros_like(note_out)
    recv[0, ctx] = send[ctx, rep]
    pl.semaphore_wait(barrier, nz * nx + reps * ny - 2)

    def note(step):
        return pltpu.make_async_remote_copy(
            src_ref=note_out, dst_ref=note_in.at[rep * ny + y],
            send_sem=note_send_sem, recv_sem=note_sem, device_id=along_column(step), device_id_type=MESH,
        )

    @pl.loop(1, reps * ny)
    def _(step):
        note(step).start()

    def send_block(phase, i, j):
        pltpu.make_async_remote_copy(
            src_ref=send.at[j, i], dst_ref=recv.at[phase, ctx],
            send_sem=send_sem, recv_sem=recv_sem.at[phase], device_id=(i, j), device_id_type=MESH,
        ).start()

    @pl.loop(1, nz * nx)
    def _(step):
        send_block(0, rep, place(z + swing(step // nx, nz), y, x + step % nx))

    @pl.loop(1, reps * ny)
    def _(step):
        phase = step // ny
        send_block(phase, peer(phase), place(z, y + step % ny, x))

    for load in loads[3:]:
        load.wait()

    for n in range(chunks):
        filter_rows[n * here:(n + 1) * here, :] = filter_ref[:, n * width:(n + 1) * width]

    count = reps * ny - 1
    pltpu.make_async_copy(note_in.at[pl.ds(0, count)], note_in.at[pl.ds(0, count)], note_sem).wait()
    pltpu.make_async_copy(note_in.at[pl.ds(0, count)], note_in.at[pl.ds(0, count)], note_send_sem).wait()

    @pl.loop(1, reps * chunks)
    def _(step):
        phase, rest = step // chunks, step % chunks
        turn_y, turn_x = rest // nz // nx, rest // nz % nx
        to_row = (phase == 0) & (turn_y == 0)
        to_column = (rest % nz == 0) & (turn_x == 0)

        @pl.when(jnp.logical_not(to_row | to_column))
        def _():
            send_block(phase, peer(phase), partner(rest))

    @pl.loop(0, here)
    def _(c):
        high, low = split(filter_rows[pl.ds(c, chunks, stride=here), :])
        section = dot(filter_first_ref[...], jnp.concatenate([high, low, high], axis=0))
        filter_spec[c] = dot3(twisted(section), second_hi_ref[...], second_lo_ref[...]) * scale
        cross[c] = jnp.zeros((chunks, 2 * width), F32)

    def convolve(phase):
        rows_in[...] = recv[phase].astype(F32).reshape(chunks * 16, width)

        @pl.loop(0, here)
        def _(c):
            value = rows_in[pl.ds(c, chunks, stride=16), :].astype(BF16)
            d_conv = rows_in[pl.ds(c + here, chunks, stride=16), :].astype(BF16)
            pair = jnp.concatenate([value, d_conv], axis=1)
            section = dot(first_ref[...], jnp.concatenate([pair, pair], axis=0))
            spectra[c] = jnp.concatenate([twisted(section[:, :width]), twisted(section[:, width:])], axis=0)

        flat = spectra[...].reshape(here * 2 * chunks, 2 * width)
        spectra[...] = dot3(flat, second_hi_ref[...], second_lo_ref[...]).reshape(spectra.shape)

        @pl.loop(0, here)
        def _(c):
            vr, vi = spectra[c, :chunks, :width], spectra[c, :chunks, width:]
            dr, di = spectra[c, chunks:, :width], spectra[c, chunks:, width:]
            fr, fi = filter_spec[c, :, :width], filter_spec[c, :, width:]
            cross[c, :, :width] += dr * vr + di * vi
            cross[c, :, width:] += di * vr - dr * vi
            spectra[c, :chunks, :width] = fr * vr - fi * vi
            spectra[c, :chunks, width:] = fr * vi + fi * vr
            spectra[c, chunks:, :width] = fr * dr + fi * di
            spectra[c, chunks:, width:] = fr * di - fi * dr

        flat = spectra[...].reshape(here * 2 * chunks, 2 * width)
        spectra[...] = dot3(flat, back_hi_ref[...], back_lo_ref[...]).reshape(spectra.shape)

        @pl.loop(0, here)
        def _(c):
            skip = skip_ref[mine + c]
            both = jnp.concatenate(
                [untwisted(spectra[c, :chunks]), untwisted(spectra[c, chunks:])], axis=1
            )
            high, low = split(both)
            parts = dot(last_ref[...], jnp.concatenate([high, low], axis=0))
            result = parts[:chunks] + parts[chunks:]
            value = rows_in[pl.ds(c, chunks, stride=16), :]
            d_conv = rows_in[pl.ds(c + here, chunks, stride=16), :]
            rows_out[pl.ds(c, chunks, stride=16), :] = result[:, :width] + skip * value
            rows_out[pl.ds(c + here, chunks, stride=16), :] = result[:, width:] + skip * d_conv

        result_out[phase] = rows_out[...].reshape(chunks, 16, width).astype(BF16)

    def send_back(phase, start):
        other = peer(phase)

        @pl.loop(start, chunks)
        def _(step):
            j = partner(step)
            pltpu.make_async_remote_copy(
                src_ref=result_out.at[phase, j], dst_ref=back.at[ctx, rep],
                send_sem=back_send_sem, recv_sem=back_sem.at[phase], device_id=(other, j), device_id_type=MESH,
            ).start()

    def wait_blocks(phase, sem):
        arrived = recv.at[phase, pl.ds(0, chunks - 1 if phase == 0 else chunks)]
        pltpu.make_async_copy(arrived, arrived, sem.at[phase]).wait()

    for phase in range(reps):
        wait_blocks(phase, recv_sem)
        if phase == reps - 1:
            for earlier in range(phase):
                send_back(earlier, 1 if earlier == 0 else 0)
        convolve(phase)
        if phase == 0:
            back[ctx, rep] = result_out[0, ctx]
    send_back(reps - 1, 0)

    factor = scale / math.sqrt(reps * chunks * width)

    @pl.loop(0, here)
    def _(c):
        both = untwisted(dot3(cross[c] * factor, back_hi_ref[...], back_lo_ref[...]))
        high, low = split(both)
        parts = dot(last_ref[...], jnp.concatenate([high, low], axis=0))
        filter_rows[pl.ds(c, chunks, stride=here), :] = parts[:chunks] + parts[chunks:]

    for n in range(chunks):
        d_filter_ref[own, n * width:(n + 1) * width] = filter_rows[n * here:(n + 1) * here, :]

    filter_copies = []
    for phase in range(1, reps):
        filter_copies.append(pltpu.make_async_remote_copy(
            src_ref=d_filter_ref.at[own], dst_ref=d_filter_ref.at[own],
            send_sem=filter_send_sem.at[phase], recv_sem=filter_sem.at[phase],
            device_id=(peer(phase), ctx), device_id_type=MESH,
        ))
        filter_copies[-1].start()

    stores = [pltpu.make_async_copy(d_filter_ref.at[own], d_filter_hbm.at[own], out_sem.at[0])]
    stores[0].start()

    for half in range(reps // 2):
        for phase in (2 * half, 2 * half + 1):
            wait_blocks(phase, back_sem)
        side = (rep // 2 + half) % 2
        rows = pl.ds(pl.multiple_of(side * 16, 16), 16)

        @pl.loop(0, chunks)
        def _(k):
            block = back[k, pl.ds(side * 2, 2)].astype(F32)
            mixed = block[:, :here].reshape(16, width)
            d_values_ref[k, rows] = block[:, here:].reshape(16, width).astype(BF16)
            d_gate_ref[k, rows] = (grad_ref[k, rows].astype(F32) * mixed).astype(BF16)

        for src, dst in ((d_values_ref, d_values_hbm), (d_gate_ref, d_gate_hbm)):
            stores.append(pltpu.make_async_copy(src.at[:, rows], dst.at[:, rows], out_sem.at[len(stores)]))
            stores[-1].start()

    for phase, copy in enumerate(filter_copies, 1):
        copy.wait()
        there = pl.ds(pl.multiple_of(peer(phase) * here, here), here)
        stores.append(pltpu.make_async_copy(d_filter_ref.at[there], d_filter_hbm.at[there], out_sem.at[len(stores)]))
        stores[-1].start()
    for store in stores:
        store.wait()
    sent = send.at[pl.ds(0, chunks - 1)]
    rest = send.at[chunks - 1, pl.ds(0, reps - 1)]
    for sem in (send_sem, back_send_sem):
        pltpu.make_async_copy(sent, sent, sem).wait()
        pltpu.make_async_copy(rest, rest, sem).wait()


def finish_kernel(parts, *refs):
    count = (len(refs) - 1) // 2
    sems = refs[-1]
    copies = []
    for n, (src, dst) in enumerate(zip(refs[:count], refs[count:-1])):
        size = src.shape[0] // parts
        for part in range(parts):
            rows = pl.ds(part * size, size)
            copies.append(pltpu.make_async_copy(src.at[rows], dst.at[rows], sems.at[n, part]))
            copies[-1].start()
    for copy in copies:
        copy.wait()


def on_device(grid, grad_out, gate, values, filters, skip):
    reps = lax.axis_size("rep")
    chunks = lax.axis_size("ctx")
    channels, width = values.shape[1:]
    hbm = pl.BlockSpec(memory_space=pl.ANY)
    grad_out, gate, values = (a.reshape(chunks, channels // chunks, width) for a in (grad_out, gate, values))
    consts = [jnp.asarray(t) for t in tables(chunks, width)]
    rows = chunks * 16
    blocks = (reps, chunks, 16, width)
    blocks_back = (chunks, reps, 16, width)
    d_values, d_gate, d_filter = pl.pallas_call(
        functools.partial(whole_kernel, reps, chunks, width, grid),
        out_shape=[
            jax.ShapeDtypeStruct(values.shape, BF16),
            jax.ShapeDtypeStruct(values.shape, BF16),
            jax.ShapeDtypeStruct(filters.shape, F32),
        ],
        in_specs=[hbm] * (5 + len(consts)),
        out_specs=[hbm] * 3,
        scratch_shapes=[
            pltpu.SMEM(skip.shape, F32),
            pltpu.VMEM(values.shape, BF16),
            pltpu.VMEM(values.shape, BF16),
            pltpu.VMEM(values.shape, BF16),
            pltpu.VMEM((8, filters.shape[1]), F32),
            *(pltpu.VMEM(c.shape, c.dtype) for c in consts),
            pltpu.VMEM(values.shape, BF16),
            pltpu.VMEM(values.shape, BF16),
            pltpu.VMEM(filters.shape, F32),
            pltpu.VMEM(blocks_back, BF16),
            pltpu.VMEM(blocks, BF16),
            pltpu.VMEM(blocks, BF16),
            pltpu.VMEM(blocks_back, BF16),
            pltpu.VMEM((rows, width), F32),
            pltpu.VMEM((rows, width), F32),
            pltpu.VMEM((chunks * 8, width), F32),
            pltpu.VMEM((8, chunks, 2 * width), F32),
            pltpu.VMEM((8, chunks, 2 * width), F32),
            pltpu.VMEM((8, 2 * chunks, 2 * width), F32),
            pltpu.VMEM((8, width), F32),
            pltpu.VMEM((reps * grid[1], 8, width), F32),
            pltpu.SemaphoreType.DMA((5 + len(consts),)),
            pltpu.SemaphoreType.DMA((2 * reps,)),
            pltpu.SemaphoreType.DMA,
            pltpu.SemaphoreType.DMA((reps,)),
            pltpu.SemaphoreType.DMA,
            pltpu.SemaphoreType.DMA((reps,)),
            pltpu.SemaphoreType.DMA((reps,)),
            pltpu.SemaphoreType.DMA((reps,)),
            pltpu.SemaphoreType.DMA,
            pltpu.SemaphoreType.DMA,
        ],
        compiler_params=pltpu.CompilerParams(
            vmem_limit_bytes=56 * 1024 * 1024, collective_id=0, has_side_effects=True
        ),
        name="whole",
    )(skip, grad_out, gate, values, filters, *consts)
    parts = 4
    results = (d_values, d_gate, d_filter)
    d_values, d_gate, d_filter = pl.pallas_call(
        functools.partial(finish_kernel, parts),
        out_shape=[jax.ShapeDtypeStruct(a.shape, a.dtype) for a in results],
        in_specs=[hbm] * 3,
        out_specs=[hbm] * 3,
        scratch_shapes=[pltpu.SemaphoreType.DMA((3, parts))],
        compiler_params=pltpu.CompilerParams(vmem_limit_bytes=56 * 1024 * 1024),
        name="finish",
    )(*results)
    return d_values.reshape(1, channels, width), d_gate.reshape(1, channels, width), d_filter


def solution(mesh):
    placed = (
        P("rep", None, "ctx"),
        P("rep", None, "ctx"),
        P("rep", None, "ctx"),
        P("ctx", None),
        P("ctx"),
    )
    grid = (mesh.shape["ctx"] // 8, 4, 2)
    return jax.shard_map(
        functools.partial(on_device, grid),
        mesh=mesh,
        in_specs=placed,
        out_specs=(P("rep", None, "ctx"), P("rep", None, "ctx"), P("ctx", None)),
        check_vma=False,
    )
```

```python
import functools
import math

import jax
import jax.numpy as jnp
import ml_dtypes
import numpy as np
from jax import lax
from jax.experimental import pallas as pl
from jax.experimental.pallas import tpu as pltpu
from jax.sharding import PartitionSpec as P

MESH = pl.DeviceIdType.MESH
F32 = jnp.float32
BF16 = jnp.bfloat16


def split_np(table):
    high = table.astype(ml_dtypes.bfloat16)
    low = (table - high.astype(np.float64)).astype(ml_dtypes.bfloat16)
    return high, low


@functools.lru_cache(None)
def tables(chunks, width):
    total = chunks * width
    n = np.arange(chunks)
    q = np.arange(width)
    outer = 2 * np.pi * np.outer(n + 0.25, n) / chunks
    turn = 2 * np.pi * np.outer(n + 0.25, q) / total
    inner = 2 * np.pi * (np.outer(q, q) % width) / width
    first = np.concatenate([np.cos(outer), -np.sin(outer)], axis=0)
    first_hi, first_lo = split_np(first)
    fwd_first = np.concatenate([first_hi, first_lo], axis=1)
    filter_first = np.concatenate([first_hi, first_hi, first_lo], axis=1)
    cos, sin = np.cos(inner), np.sin(inner)
    second = np.block([[cos, -sin], [sin, cos]])
    second_hi, second_lo = split_np(second)
    back_hi, back_lo = split_np(second.T)
    second = np.concatenate([second_hi, second_hi, second_lo], axis=0)
    back = np.concatenate([back_hi, back_hi, back_lo], axis=0)
    last = np.concatenate([np.cos(outer).T, -np.sin(outer).T], axis=1)
    last_hi, last_lo = split_np(last)
    zero = np.zeros_like(last_lo)
    inv_last = np.concatenate(
        [np.concatenate([last_hi, last_hi], axis=1), np.concatenate([last_lo, zero], axis=1)], axis=0
    )
    twist = np.stack([np.cos(turn), np.sin(turn)]).astype(np.float32)
    return fwd_first, filter_first, second, back, inv_last, twist


def dot(left, right):
    return jnp.dot(left, right, preferred_element_type=F32)


def split(array):
    high = array.astype(BF16)
    low = (array - high.astype(F32)).astype(BF16)
    return high, low


def split3(array):
    high, low = split(array)
    return jnp.concatenate([high, low, high], axis=1)


def whole_kernel(
    reps, chunks, width, grid,
    skip_hbm, grad_hbm, gate_hbm, value_hbm, filter_hbm,
    first_hbm, filter_first_hbm, second_hbm, back_hbm, last_hbm, twist_hbm,
    d_values_hbm, d_gate_hbm, d_filter_hbm,
    skip_ref, grad_ref, gate_ref, value_ref, filter_ref,
    first_ref, filter_first_ref, second_ref, back_ref, last_ref, twist_ref,
    d_values_ref, d_gate_ref, d_filter_ref,
    send, recv, result_out, back, rows_in, rows_out, filter_rows, filter_spec, cross, spectra, products, note_out, note_in,
    in_sem, out_sem,
    send_sem, recv_sem, back_send_sem, back_sem, filter_send_sem, filter_sem, note_send_sem, note_sem,
):
    here = 8
    nz, ny, nx = grid
    rep = lax.axis_index("rep")
    ctx = lax.axis_index("ctx")
    z, y, x = ctx // (ny * nx), (ctx // nx) % ny, ctx % nx
    mine = rep * here
    scale = 1.0 / (chunks * width)

    def place(zz, yy, xx):
        return (zz % nz) * (ny * nx) + (yy % ny) * nx + xx % nx

    def along_row(step):
        return rep, place(z + step // nx, y, x + step % nx)

    def along_column(step):
        return (rep + step // ny) % reps, place(z, y + step % ny, x)

    def swing(step, size):
        return (step + 1) // 2 * (2 * (step % 2) - 1) + size

    def partner(step):
        rest = step // nz
        return place(z + swing(step % nz, nz), y + swing(rest // nx, ny), x + rest % nx)

    def peer(phase):
        base = (rep + phase // 2 * 2) % reps
        return base + phase % 2 * (1 - base % 2 * 2)

    def twisted(section):
        cos, sin = twist_ref[0], twist_ref[1]
        real, imag = section[:chunks], section[chunks:]
        return jnp.concatenate([real * cos + imag * sin, imag * cos - real * sin], axis=1)

    def untwisted(section):
        cos, sin = twist_ref[0], twist_ref[1]
        real, imag = section[:, :width], section[:, width:]
        return jnp.concatenate([real * cos - imag * sin, imag * cos + real * sin], axis=0)

    own = pl.ds(pl.multiple_of(mine, here), here)
    loads = [
        pltpu.make_async_copy(src, dst, in_sem.at[n])
        for n, (src, dst) in enumerate((
            (grad_hbm, grad_ref), (gate_hbm, gate_ref), (value_hbm, value_ref),
            (filter_hbm.at[own], filter_ref), (filter_first_hbm, filter_first_ref), (twist_hbm, twist_ref),
            (second_hbm, second_ref), (first_hbm, first_ref),
            (back_hbm, back_ref), (last_hbm, last_ref), (skip_hbm, skip_ref),
        ))
    ]
    for load in loads:
        load.start()

    barrier = pltpu.get_barrier_semaphore()

    @pl.loop(1, nz * nx)
    def _(step):
        pl.semaphore_signal(barrier, 1, device_id=along_row(step), device_id_type=MESH)

    @pl.loop(1, reps * ny)
    def _(step):
        pl.semaphore_signal(barrier, 1, device_id=along_column(step), device_id_type=MESH)

    for load in loads[:3]:
        load.wait()

    @pl.loop(0, chunks)
    def _(j):
        value = value_ref[j].astype(F32)
        d_conv = grad_ref[j].astype(F32) * gate_ref[j].astype(F32)
        both = jnp.concatenate([value.reshape(reps, here, width), d_conv.reshape(reps, here, width)], axis=1)
        send[j] = both.astype(BF16)

    note_out[...] = jnp.zeros_like(note_out)
    pltpu.make_async_copy(send.at[ctx, rep], recv.at[0, ctx], recv_sem.at[0]).start()
    pl.semaphore_wait(barrier, nz * nx + reps * ny - 2)

    def note(step):
        return pltpu.make_async_remote_copy(
            src_ref=note_out, dst_ref=note_in.at[rep * ny + y],
            send_sem=note_send_sem, recv_sem=note_sem, device_id=along_column(step), device_id_type=MESH,
        )

    @pl.loop(1, reps * ny)
    def _(step):
        note(step).start()

    def send_block(phase, i, j):
        pltpu.make_async_remote_copy(
            src_ref=send.at[j, i], dst_ref=recv.at[phase, ctx],
            send_sem=send_sem, recv_sem=recv_sem.at[phase], device_id=(i, j), device_id_type=MESH,
        ).start()

    @pl.loop(1, nz * nx)
    def _(step):
        send_block(0, rep, place(z + swing(step // nx, nz), y, x + step % nx))

    @pl.loop(1, reps * ny)
    def _(step):
        phase = step // ny
        send_block(phase, peer(phase), place(z, y + step % ny, x))

    for load in loads[3:]:
        load.wait()

    for n in range(chunks):
        filter_rows[n * here:(n + 1) * here, :] = filter_ref[:, n * width:(n + 1) * width]

    count = reps * ny - 1
    pltpu.make_async_copy(note_in.at[pl.ds(0, count)], note_in.at[pl.ds(0, count)], note_sem).wait()
    pltpu.make_async_copy(note_in.at[pl.ds(0, count)], note_in.at[pl.ds(0, count)], note_send_sem).wait()

    @pl.loop(1, reps * chunks)
    def _(step):
        phase, rest = step // chunks, step % chunks
        turn_y, turn_x = rest // nz // nx, rest // nz % nx
        to_row = (phase == 0) & (turn_y == 0)
        to_column = (rest % nz == 0) & (turn_x == 0)

        @pl.when(jnp.logical_not(to_row | to_column))
        def _():
            send_block(phase, peer(phase), partner(rest))

    def last_step(both):
        high, low = split(both)
        parts = dot(last_ref[...], jnp.concatenate([high, low], axis=0))
        return parts[:chunks] + parts[chunks:]

    @pl.loop(0, here, unroll=4)
    def _(c):
        high, low = split(filter_rows[pl.ds(c, chunks, stride=here), :])
        section = dot(filter_first_ref[...], jnp.concatenate([high, low, high], axis=0))
        filter_spec[c] = dot(split3(twisted(section)), second_ref[...]) * scale
        cross[c] = jnp.zeros((chunks, 2 * width), F32)

    def to_spectra(phase):
        rows_in[...] = recv[phase].astype(F32).reshape(chunks * 16, width)

        @pl.loop(0, here, unroll=here)
        def _(c):
            value = rows_in[pl.ds(c, chunks, stride=16), :].astype(BF16)
            d_conv = rows_in[pl.ds(c + here, chunks, stride=16), :].astype(BF16)
            pair = jnp.concatenate([value, d_conv], axis=1)
            section = dot(first_ref[...], jnp.concatenate([pair, pair], axis=0))
            spectra[c, :chunks] = split3(twisted(section[:, :width]))
            spectra[c, chunks:] = split3(twisted(section[:, width:]))

        full = dot(spectra[...].reshape(here * 2 * chunks, 6 * width), second_ref[...])
        full = full.reshape(here, 2 * chunks, 2 * width)
        for c in range(here):
            vr, vi = full[c, :chunks, :width], full[c, :chunks, width:]
            dr, di = full[c, chunks:, :width], full[c, chunks:, width:]
            fr, fi = filter_spec[c, :, :width], filter_spec[c, :, width:]
            cross[c, :, :width] += dr * vr + di * vi
            cross[c, :, width:] += di * vr - dr * vi
            products[c, :chunks] = split3(jnp.concatenate([fr * vr - fi * vi, fr * vi + fi * vr], axis=1))
            products[c, chunks:] = split3(jnp.concatenate([fr * dr + fi * di, fr * di - fi * dr], axis=1))

    def from_products(phase):
        full = dot(products[...].reshape(here * 2 * chunks, 6 * width), back_ref[...])
        full = full.reshape(here, 2 * chunks, 2 * width)
        for c in range(here):
            skip = skip_ref[mine + c]
            result = last_step(jnp.concatenate([untwisted(full[c, :chunks]), untwisted(full[c, chunks:])], axis=1))
            value = rows_in[pl.ds(c, chunks, stride=16), :]
            d_conv = rows_in[pl.ds(c + here, chunks, stride=16), :]
            rows_out[pl.ds(c, chunks, stride=16), :] = result[:, :width] + skip * value
            rows_out[pl.ds(c + here, chunks, stride=16), :] = result[:, width:] + skip * d_conv
        result_out[phase] = rows_out[...].reshape(chunks, 16, width).astype(BF16)

    def send_back(phase, step):
        j = partner(step)
        pltpu.make_async_remote_copy(
            src_ref=result_out.at[phase, j], dst_ref=back.at[ctx, rep],
            send_sem=back_send_sem, recv_sem=back_sem.at[phase], device_id=(peer(phase), j), device_id_type=MESH,
        ).start()

    def wait_blocks(phase, sem):
        pltpu.make_async_copy(recv.at[phase], recv.at[phase], sem.at[phase]).wait()

    factor = scale / math.sqrt(reps * chunks * width)
    sibling = (peer(1), ctx)

    def filter_copy(n, phase, device):
        block = pl.ds(pl.multiple_of(peer(phase) * here, here), here)
        return pltpu.make_async_remote_copy(
            src_ref=d_filter_ref.at[block], dst_ref=d_filter_ref.at[block],
            send_sem=filter_send_sem.at[n], recv_sem=filter_sem.at[n], device_id=device, device_id_type=MESH,
        )

    to_sibling = filter_copy(0, 0, sibling)
    across = filter_copy(1, 0, (peer(2), ctx))
    onward = filter_copy(2, 2, sibling)

    @pl.loop(0, reps)
    def _(phase):
        wait_blocks(phase, recv_sem)
        to_spectra(phase)

        @pl.when(phase == reps - 1)
        def _():
            @pl.loop(0, here // 2, unroll=4)
            def _(g):
                both = [untwisted(dot(split3(cross[2 * g + e] * factor), back_ref[...])) for e in range(2)]
                result = last_step(jnp.concatenate(both, axis=1))
                for e in range(2):
                    filter_rows[pl.ds(2 * g + e, chunks, stride=here), :] = result[:, e * width:(e + 1) * width]

            for n in range(chunks):
                d_filter_ref[own, n * width:(n + 1) * width] = filter_rows[n * here:(n + 1) * here, :]
            across.start()
            to_sibling.start()

        from_products(phase)

        @pl.when(phase == 0)
        def _():
            pltpu.make_async_copy(result_out.at[0, ctx], back.at[ctx, rep], back_sem.at[0]).start()

        @pl.loop(jnp.where(phase == 0, 1, 0), chunks)
        def _(step):
            send_back(phase, step)


    stores = [pltpu.make_async_copy(d_filter_ref.at[own], d_filter_hbm.at[own], out_sem.at[0])]
    stores[0].start()

    for half in range(reps // 2):
        for phase in (2 * half, 2 * half + 1):
            wait_blocks(phase, back_sem)
        side = (rep // 2 + half) % 2
        rows = pl.ds(pl.multiple_of(side * 16, 16), 16)

        @pl.loop(0, chunks, unroll=4)
        def _(k):
            block = back[k, pl.ds(side * 2, 2)].astype(F32)
            mixed = block[:, :here].reshape(16, width)
            d_values_ref[k, rows] = block[:, here:].reshape(16, width).astype(BF16)
            d_gate_ref[k, rows] = (grad_ref[k, rows].astype(F32) * mixed).astype(BF16)

        for src, dst in ((d_values_ref, d_values_hbm), (d_gate_ref, d_gate_hbm)):
            stores.append(pltpu.make_async_copy(src.at[:, rows], dst.at[:, rows], out_sem.at[len(stores)]))
            stores[-1].start()
        if half == 0:
            across.wait_recv()
            onward.start()

    to_sibling.wait_recv()
    onward.wait_recv()
    for phase in range(1, reps):
        there = pl.ds(pl.multiple_of(peer(phase) * here, here), here)
        stores.append(pltpu.make_async_copy(d_filter_ref.at[there], d_filter_hbm.at[there], out_sem.at[len(stores)]))
        stores[-1].start()
    for copy in (to_sibling, across, onward):
        copy.wait_send()
    for store in stores:
        store.wait()
    sent = send.at[pl.ds(0, chunks - 1)]
    rest = send.at[chunks - 1, pl.ds(0, reps - 1)]
    for sem in (send_sem, back_send_sem):
        pltpu.make_async_copy(sent, sent, sem).wait()
        pltpu.make_async_copy(rest, rest, sem).wait()


def finish_kernel(parts, *refs):
    count = (len(refs) - 2) // 3
    sources, targets, held = refs[:count], refs[count:2 * count], refs[2 * count:3 * count]
    in_sems, out_sems = refs[-2:]
    pieces = []
    for part in range(parts):
        for n in range(count):
            size = sources[n].shape[0] // parts
            rows = pl.ds(part * size, size)
            pieces.append((
                pltpu.make_async_copy(sources[n].at[rows], held[n].at[rows], in_sems.at[n, part]),
                pltpu.make_async_copy(held[n].at[rows], targets[n].at[rows], out_sems.at[n, part]),
            ))
    for load, _ in pieces:
        load.start()
    for load, store in pieces:
        load.wait()
        store.start()
    for _, store in pieces:
        store.wait()


def on_device(grid, grad_out, gate, values, filters, skip):
    reps = lax.axis_size("rep")
    chunks = lax.axis_size("ctx")
    channels, width = values.shape[1:]
    hbm = pl.BlockSpec(memory_space=pl.ANY)
    grad_out, gate, values = (a.reshape(chunks, channels // chunks, width) for a in (grad_out, gate, values))
    consts = [jnp.asarray(t) for t in tables(chunks, width)]
    rows = chunks * 16
    blocks = (reps, chunks, 16, width)
    blocks_back = (chunks, reps, 16, width)
    d_values, d_gate, d_filter = pl.pallas_call(
        functools.partial(whole_kernel, reps, chunks, width, grid),
        out_shape=[
            jax.ShapeDtypeStruct(values.shape, BF16),
            jax.ShapeDtypeStruct(values.shape, BF16),
            jax.ShapeDtypeStruct(filters.shape, F32),
        ],
        in_specs=[hbm] * (5 + len(consts)),
        out_specs=[hbm] * 3,
        scratch_shapes=[
            pltpu.SMEM(skip.shape, F32),
            pltpu.VMEM(values.shape, BF16),
            pltpu.VMEM(values.shape, BF16),
            pltpu.VMEM(values.shape, BF16),
            pltpu.VMEM((8, filters.shape[1]), F32),
            *(pltpu.VMEM(c.shape, c.dtype) for c in consts),
            pltpu.VMEM(values.shape, BF16),
            pltpu.VMEM(values.shape, BF16),
            pltpu.VMEM(filters.shape, F32),
            pltpu.VMEM(blocks_back, BF16),
            pltpu.VMEM(blocks, BF16),
            pltpu.VMEM(blocks, BF16),
            pltpu.VMEM(blocks_back, BF16),
            pltpu.VMEM((rows, width), F32),
            pltpu.VMEM((rows, width), F32),
            pltpu.VMEM((chunks * 8, width), F32),
            pltpu.VMEM((8, chunks, 2 * width), F32),
            pltpu.VMEM((8, chunks, 2 * width), F32),
            pltpu.VMEM((8, 2 * chunks, 6 * width), BF16),
            pltpu.VMEM((8, 2 * chunks, 6 * width), BF16),
            pltpu.VMEM((8, width), F32),
            pltpu.VMEM((reps * grid[1], 8, width), F32),
            pltpu.SemaphoreType.DMA((5 + len(consts),)),
            pltpu.SemaphoreType.DMA((2 * reps,)),
            pltpu.SemaphoreType.DMA,
            pltpu.SemaphoreType.DMA((reps,)),
            pltpu.SemaphoreType.DMA,
            pltpu.SemaphoreType.DMA((reps,)),
            pltpu.SemaphoreType.DMA((reps,)),
            pltpu.SemaphoreType.DMA((reps,)),
            pltpu.SemaphoreType.DMA,
            pltpu.SemaphoreType.DMA,
        ],
        compiler_params=pltpu.CompilerParams(
            vmem_limit_bytes=56 * 1024 * 1024, collective_id=0, has_side_effects=True
        ),
        name="whole",
    )(skip, grad_out, gate, values, filters, *consts)
    parts = 4
    results = (d_values, d_gate, d_filter)
    d_values, d_gate, d_filter = pl.pallas_call(
        functools.partial(finish_kernel, parts),
        out_shape=[jax.ShapeDtypeStruct(a.shape, a.dtype) for a in results],
        in_specs=[hbm] * 3,
        out_specs=[hbm] * 3,
        scratch_shapes=[pltpu.VMEM(a.shape, a.dtype) for a in results]
        + [pltpu.SemaphoreType.DMA((3, parts))] * 2,
        compiler_params=pltpu.CompilerParams(vmem_limit_bytes=56 * 1024 * 1024),
        name="finish",
    )(*results)
    return d_values.reshape(1, channels, width), d_gate.reshape(1, channels, width), d_filter


def solution(mesh):
    placed = (
        P("rep", None, "ctx"),
        P("rep", None, "ctx"),
        P("rep", None, "ctx"),
        P("ctx", None),
        P("ctx"),
    )
    grid = (mesh.shape["ctx"] // 8, 4, 2)
    return jax.shard_map(
        functools.partial(on_device, grid),
        mesh=mesh,
        in_specs=placed,
        out_specs=(P("rep", None, "ctx"), P("rep", None, "ctx"), P("ctx", None)),
        check_vma=False,
    )
```

```python
import functools
import math

import jax
import jax.numpy as jnp
import ml_dtypes
import numpy as np
from jax import lax
from jax.experimental import pallas as pl
from jax.experimental.pallas import tpu as pltpu
from jax.sharding import PartitionSpec as P

MESH = pl.DeviceIdType.MESH
F32 = jnp.float32
BF16 = jnp.bfloat16


def split_np(table):
    high = table.astype(ml_dtypes.bfloat16)
    low = (table - high.astype(np.float64)).astype(ml_dtypes.bfloat16)
    return high, low


@functools.lru_cache(None)
def tables(chunks, width):
    total = chunks * width
    n = np.arange(chunks)
    q = np.arange(width)
    outer = 2 * np.pi * np.outer(n + 0.25, n) / chunks
    turn = 2 * np.pi * np.outer(n + 0.25, q) / total
    inner = 2 * np.pi * (np.outer(q, q) % width) / width
    first = np.concatenate([np.cos(outer), -np.sin(outer)], axis=0)
    first_hi, first_lo = split_np(first)
    fwd_first = np.concatenate([first_hi, first_lo], axis=1)
    filter_first = np.concatenate([first_hi, first_hi, first_lo], axis=1)
    cos, sin = np.cos(inner), np.sin(inner)
    second = np.block([[cos, -sin], [sin, cos]])
    second_hi, second_lo = split_np(second)
    back_hi, back_lo = split_np(second.T)
    second = np.concatenate([second_hi, second_hi, second_lo], axis=0)
    back = np.concatenate([back_hi, back_hi, back_lo], axis=0)
    last = np.concatenate([np.cos(outer).T, -np.sin(outer).T], axis=1)
    last_hi, last_lo = split_np(last)
    zero = np.zeros_like(last_lo)
    inv_last = np.concatenate(
        [np.concatenate([last_hi, last_hi], axis=1), np.concatenate([last_lo, zero], axis=1)], axis=0
    )
    twist = np.stack([np.cos(turn), np.sin(turn)]).astype(np.float32)
    return fwd_first, filter_first, second, back, inv_last, twist


def dot(left, right):
    return jnp.dot(left, right, preferred_element_type=F32)


def split(array):
    high = array.astype(BF16)
    low = (array - high.astype(F32)).astype(BF16)
    return high, low


def split3(array):
    high, low = split(array)
    return jnp.concatenate([high, low, high], axis=1)


def whole_kernel(
    reps, chunks, width, grid,
    skip_hbm, grad_hbm, gate_hbm, value_hbm, filter_hbm,
    first_hbm, filter_first_hbm, second_hbm, back_hbm, last_hbm, twist_hbm,
    d_values_hbm, d_gate_hbm, d_filter_hbm,
    skip_ref, grad_ref, gate_ref, value_ref, filter_ref,
    first_ref, filter_first_ref, second_ref, back_ref, last_ref, twist_ref,
    d_values_ref, d_gate_ref, d_filter_ref,
    send, recv, result_out, back, rows_in, rows_out, filter_rows, filter_spec, cross, spectra, products, note_out, note_in,
    in_sem, out_sem,
    send_sem, recv_sem, back_send_sem, back_sem, filter_send_sem, filter_sem, note_send_sem, note_sem,
):
    here = 8
    nz, ny, nx = grid
    rep = lax.axis_index("rep")
    ctx = lax.axis_index("ctx")
    z, y, x = lax.div(ctx, ny * nx), lax.rem(lax.div(ctx, nx), ny), lax.rem(ctx, nx)
    mine = rep * here
    scale = 1.0 / (chunks * width)

    swing_z = [0] + [d * sign for d in range(1, nz // 2) for sign in (1, -1)] + [nz // 2]
    to_z = [lax.rem(z + step + nz, nz) * (ny * nx) for step in swing_z]

    def to_yx(turn_y, turn_x):
        return lax.rem(y + turn_y, ny) * nx + lax.rem(x + turn_x, nx)

    stay = to_yx(0, 0)

    def around(start, stop, act):
        @pl.loop(start, stop)
        def _(step):
            phase, rest = lax.div(step, ny * nx), lax.rem(step, ny * nx)
            turn_x = lax.rem(rest, nx)
            there = to_yx(lax.div(rest, nx), turn_x)
            act(phase, turn_x, there)

    def along_row(act):
        for n, start in enumerate(to_z):
            for turn_x in range(nx):
                if n or turn_x:
                    act(0, start + to_yx(0, turn_x))

    def along_column(act):
        for phase in range(reps):
            for turn_y in range(ny):
                if phase or turn_y:
                    act(phase, to_z[0] + to_yx(turn_y, 0))

    def peer(phase):
        base = lax.rem(rep + lax.div(phase, 2) * 2, reps)
        return base + lax.rem(phase, 2) * (1 - lax.rem(base, 2) * 2)

    def twisted(section):
        cos, sin = twist_ref[0], twist_ref[1]
        real, imag = section[:chunks], section[chunks:]
        return jnp.concatenate([real * cos + imag * sin, imag * cos - real * sin], axis=1)

    def untwisted(section):
        cos, sin = twist_ref[0], twist_ref[1]
        real, imag = section[:, :width], section[:, width:]
        return jnp.concatenate([real * cos - imag * sin, imag * cos + real * sin], axis=0)

    own = pl.ds(pl.multiple_of(mine, here), here)
    loads = [
        pltpu.make_async_copy(src, dst, in_sem.at[n])
        for n, (src, dst) in enumerate((
            (grad_hbm, grad_ref), (gate_hbm, gate_ref), (value_hbm, value_ref),
            (filter_hbm.at[own], filter_ref), (filter_first_hbm, filter_first_ref), (twist_hbm, twist_ref),
            (second_hbm, second_ref), (first_hbm, first_ref),
            (back_hbm, back_ref), (last_hbm, last_ref), (skip_hbm, skip_ref),
        ))
    ]
    for load in loads:
        load.start()

    barrier = pltpu.get_barrier_semaphore()

    def greet(phase, j):
        pl.semaphore_signal(barrier, 1, device_id=(peer(phase), j), device_id_type=MESH)

    along_row(greet)
    along_column(greet)

    for load in loads[:3]:
        load.wait()

    @pl.loop(0, chunks, unroll=4)
    def _(j):
        value = value_ref[j].astype(F32)
        d_conv = grad_ref[j].astype(F32) * gate_ref[j].astype(F32)
        both = jnp.concatenate([value.reshape(reps, here, width), d_conv.reshape(reps, here, width)], axis=1)
        send[j] = both.astype(BF16)

    note_out[...] = jnp.zeros_like(note_out)
    pltpu.make_async_copy(send.at[ctx, rep], recv.at[0, ctx], recv_sem.at[0]).start()
    pl.semaphore_wait(barrier, nz * nx + reps * ny - 2)

    def note(phase, j):
        pltpu.make_async_remote_copy(
            src_ref=note_out, dst_ref=note_in.at[rep * ny + y],
            send_sem=note_send_sem, recv_sem=note_sem, device_id=(peer(phase), j), device_id_type=MESH,
        ).start()

    def send_block(phase, j):
        i = peer(phase)
        pltpu.make_async_remote_copy(
            src_ref=send.at[j, i], dst_ref=recv.at[phase, ctx],
            send_sem=send_sem, recv_sem=recv_sem.at[phase], device_id=(i, j), device_id_type=MESH,
        ).start()

    along_column(note)
    along_row(send_block)
    along_column(send_block)

    for load in loads[3:]:
        load.wait()

    for n in range(chunks):
        filter_rows[n * here:(n + 1) * here, :] = filter_ref[:, n * width:(n + 1) * width]

    count = reps * ny - 1
    pltpu.make_async_copy(note_in.at[pl.ds(0, count)], note_in.at[pl.ds(0, count)], note_sem).wait()
    pltpu.make_async_copy(note_in.at[pl.ds(0, count)], note_in.at[pl.ds(0, count)], note_send_sem).wait()

    def send_ring(phase, turn_x, there):
        @pl.when(turn_x > 0)
        def _():
            send_block(phase, to_z[0] + there)

        for start in to_z[1:]:
            send_block(phase, start + there)

    around(nx, reps * ny * nx, send_ring)

    def last_step(both):
        high, low = split(both)
        parts = dot(last_ref[...], jnp.concatenate([high, low], axis=0))
        return parts[:chunks] + parts[chunks:]

    @pl.loop(0, here, unroll=4)
    def _(c):
        high, low = split(filter_rows[pl.ds(c, chunks, stride=here), :])
        section = dot(filter_first_ref[...], jnp.concatenate([high, low, high], axis=0))
        filter_spec[c] = dot(split3(twisted(section)), second_ref[...]) * scale
        cross[c] = jnp.zeros((chunks, 2 * width), F32)

    def to_spectra(phase):
        rows_in[...] = recv[phase].astype(F32).reshape(chunks * 16, width)

        @pl.loop(0, here, unroll=here)
        def _(c):
            value = rows_in[pl.ds(c, chunks, stride=16), :].astype(BF16)
            d_conv = rows_in[pl.ds(c + here, chunks, stride=16), :].astype(BF16)
            pair = jnp.concatenate([value, d_conv], axis=1)
            section = dot(first_ref[...], jnp.concatenate([pair, pair], axis=0))
            spectra[c, :chunks] = split3(twisted(section[:, :width]))
            spectra[c, chunks:] = split3(twisted(section[:, width:]))

        full = dot(spectra[...].reshape(here * 2 * chunks, 6 * width), second_ref[...])
        full = full.reshape(here, 2 * chunks, 2 * width)
        for c in range(here):
            vr, vi = full[c, :chunks, :width], full[c, :chunks, width:]
            dr, di = full[c, chunks:, :width], full[c, chunks:, width:]
            fr, fi = filter_spec[c, :, :width], filter_spec[c, :, width:]
            cross[c, :, :width] += dr * vr + di * vi
            cross[c, :, width:] += di * vr - dr * vi
            products[c, :chunks] = split3(jnp.concatenate([fr * vr - fi * vi, fr * vi + fi * vr], axis=1))
            products[c, chunks:] = split3(jnp.concatenate([fr * dr + fi * di, fr * di - fi * dr], axis=1))

    def from_products(phase):
        full = dot(products[...].reshape(here * 2 * chunks, 6 * width), back_ref[...])
        full = full.reshape(here, 2 * chunks, 2 * width)
        for c in range(here):
            skip = skip_ref[mine + c]
            result = last_step(jnp.concatenate([untwisted(full[c, :chunks]), untwisted(full[c, chunks:])], axis=1))
            value = rows_in[pl.ds(c, chunks, stride=16), :]
            d_conv = rows_in[pl.ds(c + here, chunks, stride=16), :]
            rows_out[pl.ds(c, chunks, stride=16), :] = result[:, :width] + skip * value
            rows_out[pl.ds(c + here, chunks, stride=16), :] = result[:, width:] + skip * d_conv
        result_out[phase] = rows_out[...].reshape(chunks, 16, width).astype(BF16)

    def send_back(phase, j):
        pltpu.make_async_remote_copy(
            src_ref=result_out.at[phase, j], dst_ref=back.at[ctx, rep],
            send_sem=back_send_sem, recv_sem=back_sem.at[phase], device_id=(peer(phase), j), device_id_type=MESH,
        ).start()

    def send_back_ring(phase, turn_x, there):
        @pl.when((phase > 0) | (there != stay))
        def _():
            send_back(phase, to_z[0] + there)

        for start in to_z[1:]:
            send_back(phase, start + there)

    def wait_blocks(phase, sem):
        pltpu.make_async_copy(recv.at[phase], recv.at[phase], sem.at[phase]).wait()

    factor = scale / math.sqrt(reps * chunks * width)
    sibling = (peer(1), ctx)

    def filter_copy(n, phase, device):
        block = pl.ds(pl.multiple_of(peer(phase) * here, here), here)
        return pltpu.make_async_remote_copy(
            src_ref=d_filter_ref.at[block], dst_ref=d_filter_ref.at[block],
            send_sem=filter_send_sem.at[n], recv_sem=filter_sem.at[n], device_id=device, device_id_type=MESH,
        )

    to_sibling = filter_copy(0, 0, sibling)
    across = filter_copy(1, 0, (peer(2), ctx))
    onward = filter_copy(2, 2, sibling)

    @pl.loop(0, reps)
    def _(phase):
        wait_blocks(phase, recv_sem)
        to_spectra(phase)

        @pl.when(phase == reps - 1)
        def _():
            @pl.loop(0, here // 2, unroll=4)
            def _(g):
                both = [untwisted(dot(split3(cross[2 * g + e] * factor), back_ref[...])) for e in range(2)]
                result = last_step(jnp.concatenate(both, axis=1))
                for e in range(2):
                    filter_rows[pl.ds(2 * g + e, chunks, stride=here), :] = result[:, e * width:(e + 1) * width]

            for n in range(chunks):
                d_filter_ref[own, n * width:(n + 1) * width] = filter_rows[n * here:(n + 1) * here, :]
            across.start()
            to_sibling.start()

        from_products(phase)

        @pl.when(phase == 0)
        def _():
            pltpu.make_async_copy(result_out.at[0, ctx], back.at[ctx, rep], back_sem.at[0]).start()

        around(phase * (ny * nx), (phase + 1) * (ny * nx), send_back_ring)

    stores = [pltpu.make_async_copy(d_filter_ref.at[own], d_filter_hbm.at[own], out_sem.at[0])]
    stores[0].start()

    for half in range(reps // 2):
        for phase in (2 * half, 2 * half + 1):
            wait_blocks(phase, back_sem)
        side = (rep // 2 + half) % 2
        rows = pl.ds(pl.multiple_of(side * 16, 16), 16)

        @pl.loop(0, chunks, unroll=4)
        def _(k):
            block = back[k, pl.ds(side * 2, 2)].astype(F32)
            mixed = block[:, :here].reshape(16, width)
            d_values_ref[k, rows] = block[:, here:].reshape(16, width).astype(BF16)
            d_gate_ref[k, rows] = (grad_ref[k, rows].astype(F32) * mixed).astype(BF16)

        for src, dst in ((d_values_ref, d_values_hbm), (d_gate_ref, d_gate_hbm)):
            stores.append(pltpu.make_async_copy(src.at[:, rows], dst.at[:, rows], out_sem.at[len(stores)]))
            stores[-1].start()
        if half == 0:
            across.wait_recv()
            onward.start()

    to_sibling.wait_recv()
    onward.wait_recv()
    for phase in range(1, reps):
        there = pl.ds(pl.multiple_of(peer(phase) * here, here), here)
        stores.append(pltpu.make_async_copy(d_filter_ref.at[there], d_filter_hbm.at[there], out_sem.at[len(stores)]))
        stores[-1].start()
    for copy in (to_sibling, across, onward):
        copy.wait_send()
    for store in stores:
        store.wait()
    sent = send.at[pl.ds(0, chunks - 1)]
    rest = send.at[chunks - 1, pl.ds(0, reps - 1)]
    for sem in (send_sem, back_send_sem):
        pltpu.make_async_copy(sent, sent, sem).wait()
        pltpu.make_async_copy(rest, rest, sem).wait()


def finish_kernel(parts, *refs):
    count = (len(refs) - 2) // 3
    sources, targets, held = refs[:count], refs[count:2 * count], refs[2 * count:3 * count]
    in_sems, out_sems = refs[-2:]
    pieces = []
    for part in range(parts):
        for n in range(count):
            size = sources[n].shape[0] // parts
            rows = pl.ds(part * size, size)
            pieces.append((
                pltpu.make_async_copy(sources[n].at[rows], held[n].at[rows], in_sems.at[n, part]),
                pltpu.make_async_copy(held[n].at[rows], targets[n].at[rows], out_sems.at[n, part]),
            ))
    for load, _ in pieces:
        load.start()
    for load, store in pieces:
        load.wait()
        store.start()
    for _, store in pieces:
        store.wait()


def on_device(grid, grad_out, gate, values, filters, skip):
    reps = lax.axis_size("rep")
    chunks = lax.axis_size("ctx")
    channels, width = values.shape[1:]
    hbm = pl.BlockSpec(memory_space=pl.ANY)
    grad_out, gate, values = (a.reshape(chunks, channels // chunks, width) for a in (grad_out, gate, values))
    consts = [jnp.asarray(t) for t in tables(chunks, width)]
    rows = chunks * 16
    blocks = (reps, chunks, 16, width)
    blocks_back = (chunks, reps, 16, width)
    d_values, d_gate, d_filter = pl.pallas_call(
        functools.partial(whole_kernel, reps, chunks, width, grid),
        out_shape=[
            jax.ShapeDtypeStruct(values.shape, BF16),
            jax.ShapeDtypeStruct(values.shape, BF16),
            jax.ShapeDtypeStruct(filters.shape, F32),
        ],
        in_specs=[hbm] * (5 + len(consts)),
        out_specs=[hbm] * 3,
        scratch_shapes=[
            pltpu.SMEM(skip.shape, F32),
            pltpu.VMEM(values.shape, BF16),
            pltpu.VMEM(values.shape, BF16),
            pltpu.VMEM(values.shape, BF16),
            pltpu.VMEM((8, filters.shape[1]), F32),
            *(pltpu.VMEM(c.shape, c.dtype) for c in consts),
            pltpu.VMEM(values.shape, BF16),
            pltpu.VMEM(values.shape, BF16),
            pltpu.VMEM(filters.shape, F32),
            pltpu.VMEM(blocks_back, BF16),
            pltpu.VMEM(blocks, BF16),
            pltpu.VMEM(blocks, BF16),
            pltpu.VMEM(blocks_back, BF16),
            pltpu.VMEM((rows, width), F32),
            pltpu.VMEM((rows, width), F32),
            pltpu.VMEM((chunks * 8, width), F32),
            pltpu.VMEM((8, chunks, 2 * width), F32),
            pltpu.VMEM((8, chunks, 2 * width), F32),
            pltpu.VMEM((8, 2 * chunks, 6 * width), BF16),
            pltpu.VMEM((8, 2 * chunks, 6 * width), BF16),
            pltpu.VMEM((8, width), F32),
            pltpu.VMEM((reps * grid[1], 8, width), F32),
            pltpu.SemaphoreType.DMA((5 + len(consts),)),
            pltpu.SemaphoreType.DMA((2 * reps,)),
            pltpu.SemaphoreType.DMA,
            pltpu.SemaphoreType.DMA((reps,)),
            pltpu.SemaphoreType.DMA,
            pltpu.SemaphoreType.DMA((reps,)),
            pltpu.SemaphoreType.DMA((reps,)),
            pltpu.SemaphoreType.DMA((reps,)),
            pltpu.SemaphoreType.DMA,
            pltpu.SemaphoreType.DMA,
        ],
        compiler_params=pltpu.CompilerParams(
            vmem_limit_bytes=56 * 1024 * 1024, collective_id=0, has_side_effects=True
        ),
        name="whole",
    )(skip, grad_out, gate, values, filters, *consts)
    parts = 4
    results = (d_values, d_gate, d_filter)
    d_values, d_gate, d_filter = pl.pallas_call(
        functools.partial(finish_kernel, parts),
        out_shape=[jax.ShapeDtypeStruct(a.shape, a.dtype) for a in results],
        in_specs=[hbm] * 3,
        out_specs=[hbm] * 3,
        scratch_shapes=[pltpu.VMEM(a.shape, a.dtype) for a in results]
        + [pltpu.SemaphoreType.DMA((3, parts))] * 2,
        compiler_params=pltpu.CompilerParams(vmem_limit_bytes=56 * 1024 * 1024),
        name="finish",
    )(*results)
    return d_values.reshape(1, channels, width), d_gate.reshape(1, channels, width), d_filter


def solution(mesh):
    placed = (
        P("rep", None, "ctx"),
        P("rep", None, "ctx"),
        P("rep", None, "ctx"),
        P("ctx", None),
        P("ctx"),
    )
    grid = (mesh.shape["ctx"] // 8, 4, 2)
    return jax.shard_map(
        functools.partial(on_device, grid),
        mesh=mesh,
        in_specs=placed,
        out_specs=(P("rep", None, "ctx"), P("rep", None, "ctx"), P("ctx", None)),
        check_vma=False,
    )
```

```python
import functools
import math

import jax
import jax.numpy as jnp
import ml_dtypes
import numpy as np
from jax import lax
from jax.experimental import pallas as pl
from jax.experimental.pallas import tpu as pltpu
from jax.sharding import PartitionSpec as P

MESH = pl.DeviceIdType.MESH
F32 = jnp.float32
BF16 = jnp.bfloat16


def split_np(table):
    high = table.astype(ml_dtypes.bfloat16)
    low = (table - high.astype(np.float64)).astype(ml_dtypes.bfloat16)
    return high, low


@functools.lru_cache(None)
def tables(chunks, width):
    total = chunks * width
    n = np.arange(chunks)
    q = np.arange(width)
    outer = 2 * np.pi * np.outer(n + 0.25, n) / chunks
    turn = 2 * np.pi * np.outer(n + 0.25, q) / total
    inner = 2 * np.pi * (np.outer(q, q) % width) / width
    first = np.concatenate([np.cos(outer), -np.sin(outer)], axis=0)
    first_hi, first_lo = split_np(first)
    fwd_first = np.concatenate([first_hi, first_lo], axis=1)
    filter_first = np.concatenate([first_hi, first_hi, first_lo], axis=1)
    cos, sin = np.cos(inner), np.sin(inner)
    second = np.block([[cos, -sin], [sin, cos]])
    second_hi, second_lo = split_np(second)
    back_hi, back_lo = split_np(second.T)
    second = np.concatenate([second_hi, second_hi, second_lo], axis=0)
    back = np.concatenate([back_hi, back_hi, back_lo], axis=0)
    last = np.concatenate([np.cos(outer).T, -np.sin(outer).T], axis=1)
    last_hi, last_lo = split_np(last)
    zero = np.zeros_like(last_lo)
    inv_last = np.concatenate(
        [np.concatenate([last_hi, last_hi], axis=1), np.concatenate([last_lo, zero], axis=1)], axis=0
    )
    twist = np.stack([np.cos(turn), np.sin(turn)]).astype(np.float32)
    return fwd_first, filter_first, second, back, inv_last, twist


def dot(left, right):
    return jnp.dot(left, right, preferred_element_type=F32)


def split(array):
    high = array.astype(BF16)
    low = (array - high.astype(F32)).astype(BF16)
    return high, low


def split3(array):
    high, low = split(array)
    return jnp.concatenate([high, low, high], axis=1)


def whole_kernel(
    reps, chunks, width, grid,
    skip_hbm, grad_hbm, gate_hbm, value_hbm, filter_hbm,
    first_hbm, filter_first_hbm, second_hbm, back_hbm, last_hbm, twist_hbm,
    back, d_filter_hbm,
    skip_ref, grad_ref, gate_ref, value_ref, filter_ref,
    first_ref, filter_first_ref, second_ref, back_ref, last_ref, twist_ref,
    d_filter_ref,
    send, recv, result_out, rows_in, rows_out, filter_rows, filter_spec, cross, spectra, products, note_out, note_in,
    in_sem, own_sem,
    send_sem, recv_sem, back_send_sem, back_sem, filter_send_sem, filter_sem, note_send_sem, note_sem,
):
    here = 8
    nz, ny, nx = grid
    rep = lax.axis_index("rep")
    ctx = lax.axis_index("ctx")
    z, y, x = lax.div(ctx, ny * nx), lax.rem(lax.div(ctx, nx), ny), lax.rem(ctx, nx)
    mine = rep * here
    scale = 1.0 / (chunks * width)

    swing_z = [0] + [d * sign for d in range(1, nz // 2) for sign in (1, -1)] + [nz // 2]
    to_z = [lax.rem(z + step + nz, nz) * (ny * nx) for step in swing_z]

    def to_yx(turn_y, turn_x):
        return lax.rem(y + turn_y, ny) * nx + lax.rem(x + turn_x, nx)

    stay = to_yx(0, 0)

    def around(start, stop, act):
        @pl.loop(start, stop)
        def _(step):
            phase, rest = lax.div(step, ny * nx), lax.rem(step, ny * nx)
            turn_x = lax.rem(rest, nx)
            there = to_yx(lax.div(rest, nx), turn_x)
            act(phase, turn_x, there)

    def along_row(act):
        for n, start in enumerate(to_z):
            for turn_x in range(nx):
                if n or turn_x:
                    act(0, start + to_yx(0, turn_x))

    def along_column(act):
        for phase in range(reps):
            for turn_y in range(ny):
                if phase or turn_y:
                    act(phase, to_z[0] + to_yx(turn_y, 0))

    def peer(phase):
        base = lax.rem(rep + lax.div(phase, 2) * 2, reps)
        return base + lax.rem(phase, 2) * (1 - lax.rem(base, 2) * 2)

    def twisted(section):
        cos, sin = twist_ref[0], twist_ref[1]
        real, imag = section[:chunks], section[chunks:]
        return jnp.concatenate([real * cos + imag * sin, imag * cos - real * sin], axis=1)

    def untwisted(section):
        cos, sin = twist_ref[0], twist_ref[1]
        real, imag = section[:, :width], section[:, width:]
        return jnp.concatenate([real * cos - imag * sin, imag * cos + real * sin], axis=0)

    own = pl.ds(pl.multiple_of(mine, here), here)
    loads = [
        pltpu.make_async_copy(src, dst, in_sem.at[n])
        for n, (src, dst) in enumerate((
            (grad_hbm, grad_ref), (gate_hbm, gate_ref), (value_hbm, value_ref),
            (filter_hbm.at[own], filter_ref), (filter_first_hbm, filter_first_ref), (twist_hbm, twist_ref),
            (second_hbm, second_ref), (first_hbm, first_ref),
            (back_hbm, back_ref), (last_hbm, last_ref), (skip_hbm, skip_ref),
        ))
    ]
    for load in loads:
        load.start()

    barrier = pltpu.get_barrier_semaphore()

    def greet(phase, j):
        pl.semaphore_signal(barrier, 1, device_id=(peer(phase), j), device_id_type=MESH)

    along_row(greet)
    along_column(greet)

    for load in loads[:3]:
        load.wait()

    @pl.loop(0, chunks, unroll=4)
    def _(j):
        value = value_ref[j].astype(F32)
        d_conv = grad_ref[j].astype(F32) * gate_ref[j].astype(F32)
        both = jnp.concatenate([value.reshape(reps, here, width), d_conv.reshape(reps, here, width)], axis=1)
        send[j] = both.astype(BF16)

    note_out[...] = jnp.zeros_like(note_out)
    pltpu.make_async_copy(send.at[ctx, rep], recv.at[0, ctx], recv_sem.at[0]).start()
    pl.semaphore_wait(barrier, nz * nx + reps * ny - 2)

    def note(phase, j):
        pltpu.make_async_remote_copy(
            src_ref=note_out, dst_ref=note_in.at[rep * ny + y],
            send_sem=note_send_sem, recv_sem=note_sem.at[rep * ny + y],
            device_id=(peer(phase), j), device_id_type=MESH,
        ).start()

    def send_block(phase, j):
        i = peer(phase)
        pltpu.make_async_remote_copy(
            src_ref=send.at[j, i], dst_ref=recv.at[phase, ctx],
            send_sem=send_sem, recv_sem=recv_sem.at[phase], device_id=(i, j), device_id_type=MESH,
        ).start()

    along_column(note)
    along_row(send_block)
    along_column(send_block)

    for load in loads[3:]:
        load.wait()

    for n in range(chunks):
        filter_rows[n * here:(n + 1) * here, :] = filter_ref[:, n * width:(n + 1) * width]

    @pl.loop(1, reps * ny)
    def _(step):
        there = lax.rem(step, ny)
        sender = peer(lax.div(step, ny)) * ny + lax.rem(y + there, ny)
        pltpu.make_async_copy(note_in.at[sender], note_in.at[sender], note_sem.at[sender]).wait()
        for turn_x in range(nx):
            for start in to_z[0 if turn_x else 1:]:
                send_block(lax.div(step, ny), start + to_yx(there, turn_x))


    def last_step(both):
        high, low = split(both)
        parts = dot(last_ref[...], jnp.concatenate([high, low], axis=0))
        return parts[:chunks] + parts[chunks:]

    @pl.loop(0, here, unroll=4)
    def _(c):
        high, low = split(filter_rows[pl.ds(c, chunks, stride=here), :])
        section = dot(filter_first_ref[...], jnp.concatenate([high, low, high], axis=0))
        filter_spec[c] = dot(split3(twisted(section)), second_ref[...]) * scale
        cross[c] = jnp.zeros((chunks, 2 * width), F32)

    def to_spectra(phase):
        rows_in[...] = recv[phase].astype(F32).reshape(chunks * 16, width)

        @pl.loop(0, here, unroll=here)
        def _(c):
            value = rows_in[pl.ds(c, chunks, stride=16), :].astype(BF16)
            d_conv = rows_in[pl.ds(c + here, chunks, stride=16), :].astype(BF16)
            pair = jnp.concatenate([value, d_conv], axis=1)
            section = dot(first_ref[...], jnp.concatenate([pair, pair], axis=0))
            spectra[c, :chunks] = split3(twisted(section[:, :width]))
            spectra[c, chunks:] = split3(twisted(section[:, width:]))

        full = dot(spectra[...].reshape(here * 2 * chunks, 6 * width), second_ref[...])
        full = full.reshape(here, 2 * chunks, 2 * width)
        for c in range(here):
            vr, vi = full[c, :chunks, :width], full[c, :chunks, width:]
            dr, di = full[c, chunks:, :width], full[c, chunks:, width:]
            fr, fi = filter_spec[c, :, :width], filter_spec[c, :, width:]
            cross[c, :, :width] += dr * vr + di * vi
            cross[c, :, width:] += di * vr - dr * vi
            products[c, :chunks] = split3(jnp.concatenate([fr * vr - fi * vi, fr * vi + fi * vr], axis=1))
            products[c, chunks:] = split3(jnp.concatenate([fr * dr + fi * di, fr * di - fi * dr], axis=1))

    def from_products(phase):
        full = dot(products[...].reshape(here * 2 * chunks, 6 * width), back_ref[...])
        full = full.reshape(here, 2 * chunks, 2 * width)
        for c in range(here):
            skip = skip_ref[mine + c]
            result = last_step(jnp.concatenate([untwisted(full[c, :chunks]), untwisted(full[c, chunks:])], axis=1))
            value = rows_in[pl.ds(c, chunks, stride=16), :]
            d_conv = rows_in[pl.ds(c + here, chunks, stride=16), :]
            rows_out[pl.ds(c, chunks, stride=16), :] = result[:, :width] + skip * value
            rows_out[pl.ds(c + here, chunks, stride=16), :] = result[:, width:] + skip * d_conv
        result_out[phase] = rows_out[...].reshape(chunks, 16, width).astype(BF16)

    def send_back(phase, j):
        pltpu.make_async_remote_copy(
            src_ref=result_out.at[phase, j], dst_ref=back.at[ctx, rep],
            send_sem=back_send_sem, recv_sem=back_sem.at[phase], device_id=(peer(phase), j), device_id_type=MESH,
        ).start()

    def send_back_ring(phase, turn_x, there):
        @pl.when((phase > 0) | (there != stay))
        def _():
            send_back(phase, to_z[0] + there)

        for start in to_z[1:]:
            send_back(phase, start + there)

    def wait_blocks(phase, sem):
        pltpu.make_async_copy(recv.at[phase], recv.at[phase], sem.at[phase]).wait()

    factor = scale / math.sqrt(reps * chunks * width)
    sibling = (peer(1), ctx)

    def filter_copy(n, src, phase, device):
        block = pl.ds(pl.multiple_of(peer(phase) * here, here), here)
        return pltpu.make_async_remote_copy(
            src_ref=src if phase == 0 else src.at[block], dst_ref=d_filter_hbm.at[block],
            send_sem=filter_send_sem.at[n], recv_sem=filter_sem.at[n], device_id=device, device_id_type=MESH,
        )

    to_sibling = filter_copy(0, d_filter_ref, 0, sibling)
    across = filter_copy(1, d_filter_ref, 0, (peer(2), ctx))
    onward = filter_copy(2, d_filter_hbm, 2, sibling)
    own_store = pltpu.make_async_copy(d_filter_ref, d_filter_hbm.at[own], own_sem)

    @pl.loop(0, reps)
    def _(phase):
        wait_blocks(phase, recv_sem)
        to_spectra(phase)

        @pl.when(phase == reps - 1)
        def _():
            @pl.loop(0, here // 2, unroll=4)
            def _(g):
                both = [untwisted(dot(split3(cross[2 * g + e] * factor), back_ref[...])) for e in range(2)]
                result = last_step(jnp.concatenate(both, axis=1))
                for e in range(2):
                    filter_rows[pl.ds(2 * g + e, chunks, stride=here), :] = result[:, e * width:(e + 1) * width]

            for n in range(chunks):
                d_filter_ref[:, n * width:(n + 1) * width] = filter_rows[n * here:(n + 1) * here, :]
            across.start()
            to_sibling.start()
            own_store.start()

        from_products(phase)

        @pl.when(phase == 0)
        def _():
            pltpu.make_async_copy(result_out.at[0, ctx], back.at[ctx, rep], back_sem.at[0]).start()

        around(phase * (ny * nx), (phase + 1) * (ny * nx), send_back_ring)

    for phase in range(reps // 2):
        wait_blocks(phase, back_sem)
    across.wait_recv()
    onward.start()
    for phase in range(reps // 2, reps):
        wait_blocks(phase, back_sem)
    to_sibling.wait_recv()
    onward.wait_recv()
    own_store.wait()
    for copy in (to_sibling, across, onward):
        copy.wait_send()
    notes = note_in.at[pl.ds(0, reps * ny - 1)]
    pltpu.make_async_copy(notes, notes, note_send_sem).wait()
    sent = send.at[pl.ds(0, chunks - 1)]
    rest = send.at[chunks - 1, pl.ds(0, reps - 1)]
    for sem in (send_sem, back_send_sem):
        pltpu.make_async_copy(sent, sent, sem).wait()
        pltpu.make_async_copy(rest, rest, sem).wait()


def finish_kernel(
    parts, back_hbm, grad_hbm, filter_hbm, d_values_hbm, d_gate_hbm, d_filter_hbm,
    back, grad, kept, d_values, d_gate, in_sem, out_sem,
):
    chunks, reps, rows, width = back.shape
    here = rows // 2
    size, kept_size = chunks // parts, kept.shape[0] // parts
    loads, stores = [], []
    for part in range(parts):
        cut, kept_cut = pl.ds(part * size, size), pl.ds(part * kept_size, kept_size)
        loads.append([
            pltpu.make_async_copy(src.at[c], dst.at[c], in_sem.at[n, part])
            for n, (src, dst, c) in enumerate(((back_hbm, back, cut), (grad_hbm, grad, cut), (filter_hbm, kept, kept_cut)))
        ])
        stores.append([
            pltpu.make_async_copy(src.at[c], dst.at[c], out_sem.at[n, part])
            for n, (src, dst, c) in enumerate((
                (d_values, d_values_hbm, cut), (d_gate, d_gate_hbm, cut), (kept, d_filter_hbm, kept_cut)
            ))
        ])
        for load in loads[-1]:
            load.start()
    for part in range(parts):
        loads[part][0].wait()
        loads[part][1].wait()

        @pl.loop(part * size, (part + 1) * size, unroll=4)
        def _(k):
            block = back[k].astype(F32)
            mixed = block[:, :here].reshape(reps * here, width)
            d_values[k] = block[:, here:].reshape(reps * here, width).astype(BF16)
            d_gate[k] = (grad[k].astype(F32) * mixed).astype(BF16)

        stores[part][0].start()
        stores[part][1].start()
        loads[part][2].wait()
        stores[part][2].start()
    for group in stores:
        for store in group:
            store.wait()


def on_device(grid, grad_out, gate, values, filters, skip):
    reps = lax.axis_size("rep")
    chunks = lax.axis_size("ctx")
    channels, width = values.shape[1:]
    hbm = pl.BlockSpec(memory_space=pl.ANY)
    grad_out, gate, values = (a.reshape(chunks, channels // chunks, width) for a in (grad_out, gate, values))
    consts = [jnp.asarray(t) for t in tables(chunks, width)]
    rows = chunks * 16
    blocks = (reps, chunks, 16, width)
    blocks_back = (chunks, reps, 16, width)
    back, d_filter = pl.pallas_call(
        functools.partial(whole_kernel, reps, chunks, width, grid),
        out_shape=[
            jax.ShapeDtypeStruct(blocks_back, BF16),
            jax.ShapeDtypeStruct(filters.shape, F32),
        ],
        in_specs=[hbm] * (5 + len(consts)),
        out_specs=[hbm] * 2,
        scratch_shapes=[
            pltpu.SMEM(skip.shape, F32),
            pltpu.VMEM(values.shape, BF16),
            pltpu.VMEM(values.shape, BF16),
            pltpu.VMEM(values.shape, BF16),
            pltpu.VMEM((8, filters.shape[1]), F32),
            *(pltpu.VMEM(c.shape, c.dtype) for c in consts),
            pltpu.VMEM((8, filters.shape[1]), F32),
            pltpu.VMEM(blocks_back, BF16),
            pltpu.VMEM(blocks, BF16),
            pltpu.VMEM(blocks, BF16),
            pltpu.VMEM((rows, width), F32),
            pltpu.VMEM((rows, width), F32),
            pltpu.VMEM((chunks * 8, width), F32),
            pltpu.VMEM((8, chunks, 2 * width), F32),
            pltpu.VMEM((8, chunks, 2 * width), F32),
            pltpu.VMEM((8, 2 * chunks, 6 * width), BF16),
            pltpu.VMEM((8, 2 * chunks, 6 * width), BF16),
            pltpu.VMEM((8, width), F32),
            pltpu.VMEM((reps * grid[1], 8, width), F32),
            pltpu.SemaphoreType.DMA((5 + len(consts),)),
            pltpu.SemaphoreType.DMA,
            pltpu.SemaphoreType.DMA,
            pltpu.SemaphoreType.DMA((reps,)),
            pltpu.SemaphoreType.DMA,
            pltpu.SemaphoreType.DMA((reps,)),
            pltpu.SemaphoreType.DMA((reps,)),
            pltpu.SemaphoreType.DMA((reps,)),
            pltpu.SemaphoreType.DMA,
            pltpu.SemaphoreType.DMA((reps * grid[1],)),
        ],
        compiler_params=pltpu.CompilerParams(
            vmem_limit_bytes=56 * 1024 * 1024, collective_id=0, has_side_effects=True
        ),
        name="whole",
    )(skip, grad_out, gate, values, filters, *consts)
    parts = 4
    d_values, d_gate, d_filter = pl.pallas_call(
        functools.partial(finish_kernel, parts),
        out_shape=[
            jax.ShapeDtypeStruct(values.shape, BF16),
            jax.ShapeDtypeStruct(values.shape, BF16),
            jax.ShapeDtypeStruct(filters.shape, F32),
        ],
        in_specs=[hbm] * 3,
        out_specs=[hbm] * 3,
        scratch_shapes=[
            pltpu.VMEM(blocks_back, BF16),
            pltpu.VMEM(values.shape, BF16),
            pltpu.VMEM(filters.shape, F32),
            pltpu.VMEM(values.shape, BF16),
            pltpu.VMEM(values.shape, BF16),
            pltpu.SemaphoreType.DMA((3, parts)),
            pltpu.SemaphoreType.DMA((3, parts)),
        ],
        compiler_params=pltpu.CompilerParams(vmem_limit_bytes=56 * 1024 * 1024),
        name="finish",
    )(back, grad_out, d_filter)
    return d_values.reshape(1, channels, width), d_gate.reshape(1, channels, width), d_filter


def solution(mesh):
    placed = (
        P("rep", None, "ctx"),
        P("rep", None, "ctx"),
        P("rep", None, "ctx"),
        P("ctx", None),
        P("ctx"),
    )
    grid = (mesh.shape["ctx"] // 8, 4, 2)
    return jax.shard_map(
        functools.partial(on_device, grid),
        mesh=mesh,
        in_specs=placed,
        out_specs=(P("rep", None, "ctx"), P("rep", None, "ctx"), P("ctx", None)),
        check_vma=False,
    )
```

```python
import functools
import math

import jax
import jax.numpy as jnp
import ml_dtypes
import numpy as np
from jax import lax
from jax.experimental import pallas as pl
from jax.experimental.pallas import tpu as pltpu
from jax.sharding import PartitionSpec as P

MESH = pl.DeviceIdType.MESH
F32 = jnp.float32
BF16 = jnp.bfloat16


def split_np(table):
    high = table.astype(ml_dtypes.bfloat16)
    low = (table - high.astype(np.float64)).astype(ml_dtypes.bfloat16)
    return high, low


@functools.lru_cache(None)
def tables(chunks, width):
    total = chunks * width
    n = np.arange(chunks)
    q = np.arange(width)
    outer = 2 * np.pi * np.outer(n + 0.25, n) / chunks
    turn = 2 * np.pi * np.outer(n + 0.25, q) / total
    inner = 2 * np.pi * (np.outer(q, q) % width) / width
    first = np.concatenate([np.cos(outer), -np.sin(outer)], axis=0)
    first_hi, first_lo = split_np(first)
    fwd_first = np.concatenate([first_hi, first_lo], axis=1)
    filter_first = np.concatenate([first_hi, first_hi, first_lo], axis=1)
    cos, sin = np.cos(inner), np.sin(inner)
    second = np.block([[cos, -sin], [sin, cos]])
    second_hi, second_lo = split_np(second)
    back_hi, back_lo = split_np(second.T)
    second = np.concatenate([second_hi, second_hi, second_lo], axis=0)
    back = np.concatenate([back_hi, back_hi, back_lo], axis=0)
    last = np.concatenate([np.cos(outer).T, -np.sin(outer).T], axis=1)
    last_hi, last_lo = split_np(last)
    zero = np.zeros_like(last_lo)
    inv_last = np.concatenate(
        [np.concatenate([last_hi, last_hi], axis=1), np.concatenate([last_lo, zero], axis=1)], axis=0
    )
    twist = np.stack([np.cos(turn), np.sin(turn)]).astype(np.float32)
    return fwd_first, filter_first, second, back, inv_last, twist


def dot(left, right):
    return jnp.dot(left, right, preferred_element_type=F32)


def split(array):
    high = array.astype(BF16)
    low = (array - high.astype(F32)).astype(BF16)
    return high, low


def split3(array):
    high, low = split(array)
    return jnp.concatenate([high, low, high], axis=1)


def whole_kernel(
    reps, chunks, width, grid,
    skip_hbm, grad_hbm, gate_hbm, value_hbm, filter_hbm,
    first_hbm, filter_first_hbm, second_hbm, back_hbm, last_hbm, twist_hbm,
    back, d_filter_hbm,
    skip_ref, grad_ref, gate_ref, value_ref, filter_ref,
    first_ref, filter_first_ref, second_ref, back_ref, last_ref, twist_ref,
    d_filter_ref,
    send, recv, result_out, rows_in, rows_out, filter_rows, filter_spec, cross, spectra, products, note_out, note_in,
    in_sem, own_sem,
    send_sem, recv_sem, back_send_sem, back_sem, filter_send_sem, filter_sem, note_send_sem, note_sem,
):
    here = 8
    nz, ny, nx = grid
    rep = lax.axis_index("rep")
    ctx = lax.axis_index("ctx")
    z, y, x = lax.div(ctx, ny * nx), lax.rem(lax.div(ctx, nx), ny), lax.rem(ctx, nx)
    mine = rep * here
    scale = 1.0 / (chunks * width)

    swing_z = [0] + [d * sign for d in range(1, nz // 2) for sign in (1, -1)] + [nz // 2]
    to_z = [lax.rem(z + step + nz, nz) * (ny * nx) for step in swing_z]

    def to_yx(turn_y, turn_x):
        return lax.rem(y + turn_y, ny) * nx + lax.rem(x + turn_x, nx)

    stay = to_yx(0, 0)

    def around(start, stop, act):
        @pl.loop(start, stop)
        def _(step):
            phase, rest = lax.div(step, ny * nx), lax.rem(step, ny * nx)
            turn_x = lax.rem(rest, nx)
            there = to_yx(lax.div(rest, nx), turn_x)
            act(phase, turn_x, there)

    tiers = ((0, 1), (1, nz))

    def early_first(act):
        for low, high in tiers:
            @pl.loop(0, ny * nx)
            def _(rest):
                there = to_yx(lax.div(rest, nx), lax.rem(rest, nx))
                if high == low + 1:
                    act(low * (ny * nx) + there)
                else:
                    for start in to_z:
                        @pl.when((start >= low * (ny * nx)) & (start < high * (ny * nx)))
                        def _():
                            act(start + there)

    def along_row(act):
        for n, start in enumerate(to_z):
            for turn_x in range(nx):
                if n or turn_x:
                    act(0, start + to_yx(0, turn_x))

    def along_column(act):
        for phase in range(reps):
            for turn_y in range(ny):
                if phase or turn_y:
                    act(phase, to_z[0] + to_yx(turn_y, 0))

    def peer(phase):
        base = lax.rem(rep + lax.div(phase, 2) * 2, reps)
        return base + lax.rem(phase, 2) * (1 - lax.rem(base, 2) * 2)

    def twisted(section):
        cos, sin = twist_ref[0], twist_ref[1]
        real, imag = section[:chunks], section[chunks:]
        return jnp.concatenate([real * cos + imag * sin, imag * cos - real * sin], axis=1)

    def untwisted(section):
        cos, sin = twist_ref[0], twist_ref[1]
        real, imag = section[:, :width], section[:, width:]
        return jnp.concatenate([real * cos - imag * sin, imag * cos + real * sin], axis=0)

    own = pl.ds(pl.multiple_of(mine, here), here)
    loads = [
        pltpu.make_async_copy(src, dst, in_sem.at[n])
        for n, (src, dst) in enumerate((
            (grad_hbm, grad_ref), (gate_hbm, gate_ref), (value_hbm, value_ref),
            (filter_hbm.at[own], filter_ref), (filter_first_hbm, filter_first_ref), (twist_hbm, twist_ref),
            (second_hbm, second_ref), (first_hbm, first_ref),
            (back_hbm, back_ref), (last_hbm, last_ref), (skip_hbm, skip_ref),
        ))
    ]
    for load in loads:
        load.start()

    barrier = pltpu.get_barrier_semaphore()

    def greet(phase, j):
        pl.semaphore_signal(barrier, 1, device_id=(peer(phase), j), device_id_type=MESH)

    along_row(greet)
    along_column(greet)

    for load in loads[:3]:
        load.wait()

    @pl.loop(0, chunks, unroll=4)
    def _(j):
        value = value_ref[j].astype(F32)
        d_conv = grad_ref[j].astype(F32) * gate_ref[j].astype(F32)
        both = jnp.concatenate([value.reshape(reps, here, width), d_conv.reshape(reps, here, width)], axis=1)
        send[j] = both.astype(BF16)

    note_out[...] = jnp.zeros_like(note_out)
    pltpu.make_async_copy(send.at[ctx, rep], recv.at[0, ctx], recv_sem.at[0]).start()
    pl.semaphore_wait(barrier, nz * nx + reps * ny - 2)

    def note(phase, j):
        pltpu.make_async_remote_copy(
            src_ref=note_out, dst_ref=note_in.at[rep * ny + y],
            send_sem=note_send_sem, recv_sem=note_sem.at[rep * ny + y],
            device_id=(peer(phase), j), device_id_type=MESH,
        ).start()

    def send_block(phase, j):
        i = peer(phase)
        pltpu.make_async_remote_copy(
            src_ref=send.at[j, i], dst_ref=recv.at[phase, ctx],
            send_sem=send_sem, recv_sem=recv_sem.at[phase], device_id=(i, j), device_id_type=MESH,
        ).start()

    along_column(note)
    along_row(send_block)
    along_column(send_block)

    @pl.loop(1, reps * ny)
    def _(step):
        there = lax.rem(step, ny)
        sender = peer(lax.div(step, ny)) * ny + lax.rem(y + there, ny)
        pltpu.make_async_copy(note_in.at[sender], note_in.at[sender], note_sem.at[sender]).wait()
        for turn_x in range(nx):
            for start in to_z[0 if turn_x else 1:]:
                send_block(lax.div(step, ny), start + to_yx(there, turn_x))


    for load in loads[3:]:
        load.wait()

    for n in range(chunks):
        filter_rows[n * here:(n + 1) * here, :] = filter_ref[:, n * width:(n + 1) * width]

    def last_step(both):
        high, low = split(both)
        parts = dot(last_ref[...], jnp.concatenate([high, low], axis=0))
        return parts[:chunks] + parts[chunks:]

    @pl.loop(0, here, unroll=4)
    def _(c):
        high, low = split(filter_rows[pl.ds(c, chunks, stride=here), :])
        section = dot(filter_first_ref[...], jnp.concatenate([high, low, high], axis=0))
        filter_spec[c] = dot(split3(twisted(section)), second_ref[...]) * scale
        cross[c] = jnp.zeros((chunks, 2 * width), F32)

    def to_spectra(phase):
        rows_in[...] = recv[phase].astype(F32).reshape(chunks * 16, width)

        @pl.loop(0, here, unroll=here)
        def _(c):
            value = rows_in[pl.ds(c, chunks, stride=16), :].astype(BF16)
            d_conv = rows_in[pl.ds(c + here, chunks, stride=16), :].astype(BF16)
            pair = jnp.concatenate([value, d_conv], axis=1)
            section = dot(first_ref[...], jnp.concatenate([pair, pair], axis=0))
            spectra[c, :chunks] = split3(twisted(section[:, :width]))
            spectra[c, chunks:] = split3(twisted(section[:, width:]))

        full = dot(spectra[...].reshape(here * 2 * chunks, 6 * width), second_ref[...])
        full = full.reshape(here, 2 * chunks, 2 * width)
        for c in range(here):
            vr, vi = full[c, :chunks, :width], full[c, :chunks, width:]
            dr, di = full[c, chunks:, :width], full[c, chunks:, width:]
            fr, fi = filter_spec[c, :, :width], filter_spec[c, :, width:]
            cross[c, :, :width] += dr * vr + di * vi
            cross[c, :, width:] += di * vr - dr * vi
            products[c, :chunks] = split3(jnp.concatenate([fr * vr - fi * vi, fr * vi + fi * vr], axis=1))
            products[c, chunks:] = split3(jnp.concatenate([fr * dr + fi * di, fr * di - fi * dr], axis=1))

    def from_products(phase):
        full = dot(products[...].reshape(here * 2 * chunks, 6 * width), back_ref[...])
        full = full.reshape(here, 2 * chunks, 2 * width)
        for c in range(here):
            skip = skip_ref[mine + c]
            result = last_step(jnp.concatenate([untwisted(full[c, :chunks]), untwisted(full[c, chunks:])], axis=1))
            value = rows_in[pl.ds(c, chunks, stride=16), :]
            d_conv = rows_in[pl.ds(c + here, chunks, stride=16), :]
            rows_out[pl.ds(c, chunks, stride=16), :] = result[:, :width] + skip * value
            rows_out[pl.ds(c + here, chunks, stride=16), :] = result[:, width:] + skip * d_conv
        result_out[phase] = rows_out[...].reshape(chunks, 16, width).astype(BF16)

    def send_back(phase, j):
        pltpu.make_async_remote_copy(
            src_ref=result_out.at[phase, j], dst_ref=back.at[ctx, rep],
            send_sem=back_send_sem, recv_sem=back_sem.at[phase], device_id=(peer(phase), j), device_id_type=MESH,
        ).start()

    def send_back_ring(phase, turn_x, there):
        @pl.when((phase > 0) | (there != stay))
        def _():
            send_back(phase, to_z[0] + there)

        for start in to_z[1:]:
            send_back(phase, start + there)

    def wait_blocks(phase, sem):
        pltpu.make_async_copy(recv.at[phase], recv.at[phase], sem.at[phase]).wait()

    factor = scale / math.sqrt(reps * chunks * width)
    sibling = (peer(1), ctx)

    def filter_copy(n, src, phase, device):
        block = pl.ds(pl.multiple_of(peer(phase) * here, here), here)
        return pltpu.make_async_remote_copy(
            src_ref=src if phase == 0 else src.at[block], dst_ref=d_filter_hbm.at[block],
            send_sem=filter_send_sem.at[n], recv_sem=filter_sem.at[n], device_id=device, device_id_type=MESH,
        )

    to_sibling = filter_copy(0, d_filter_ref, 0, sibling)
    across = filter_copy(1, d_filter_ref, 0, (peer(2), ctx))
    onward = filter_copy(2, d_filter_hbm, 2, sibling)
    own_store = pltpu.make_async_copy(d_filter_ref, d_filter_hbm.at[own], own_sem)

    @pl.loop(0, reps)
    def _(phase):
        wait_blocks(phase, recv_sem)
        to_spectra(phase)

        @pl.when(phase == reps - 1)
        def _():
            @pl.loop(0, here // 2, unroll=4)
            def _(g):
                both = [untwisted(dot(split3(cross[2 * g + e] * factor), back_ref[...])) for e in range(2)]
                result = last_step(jnp.concatenate(both, axis=1))
                for e in range(2):
                    filter_rows[pl.ds(2 * g + e, chunks, stride=here), :] = result[:, e * width:(e + 1) * width]

            for n in range(chunks):
                d_filter_ref[:, n * width:(n + 1) * width] = filter_rows[n * here:(n + 1) * here, :]
            across.start()
            to_sibling.start()
            own_store.start()

        from_products(phase)

        @pl.when(phase == 0)
        def _():
            pltpu.make_async_copy(result_out.at[0, ctx], back.at[ctx, rep], back_sem.at[0]).start()

        @pl.when(phase < reps - 1)
        def _():
            around(phase * (ny * nx), (phase + 1) * (ny * nx), send_back_ring)

        @pl.when(phase == reps - 1)
        def _():
            early_first(lambda j: send_back(reps - 1, j))

    for phase in range(reps // 2):
        wait_blocks(phase, back_sem)
    across.wait_recv()
    onward.start()
    for phase in range(reps // 2, reps):
        wait_blocks(phase, back_sem)
    to_sibling.wait_recv()
    onward.wait_recv()
    own_store.wait()
    for copy in (to_sibling, across, onward):
        copy.wait_send()
    notes = note_in.at[pl.ds(0, reps * ny - 1)]
    pltpu.make_async_copy(notes, notes, note_send_sem).wait()
    sent = send.at[pl.ds(0, chunks - 1)]
    rest = send.at[chunks - 1, pl.ds(0, reps - 1)]
    for sem in (send_sem, back_send_sem):
        pltpu.make_async_copy(sent, sent, sem).wait()
        pltpu.make_async_copy(rest, rest, sem).wait()


def finish_kernel(
    parts, back_hbm, grad_hbm, filter_hbm, d_values_hbm, d_gate_hbm, d_filter_hbm,
    back, grad, kept, d_values, d_gate, in_sem, out_sem,
):
    chunks, reps, rows, width = back.shape
    here = rows // 2
    size, kept_size = chunks // parts, kept.shape[0] // parts
    loads, stores = [], []
    for part in range(parts):
        cut, kept_cut = pl.ds(part * size, size), pl.ds(part * kept_size, kept_size)
        loads.append([
            pltpu.make_async_copy(src.at[c], dst.at[c], in_sem.at[n, part])
            for n, (src, dst, c) in enumerate(((back_hbm, back, cut), (grad_hbm, grad, cut), (filter_hbm, kept, kept_cut)))
        ])
        stores.append([
            pltpu.make_async_copy(src.at[c], dst.at[c], out_sem.at[n, part])
            for n, (src, dst, c) in enumerate((
                (d_values, d_values_hbm, cut), (d_gate, d_gate_hbm, cut), (kept, d_filter_hbm, kept_cut)
            ))
        ])
        for load in loads[-1]:
            load.start()
    for part in range(parts):
        loads[part][0].wait()
        loads[part][1].wait()

        @pl.loop(part * size, (part + 1) * size, unroll=4)
        def _(k):
            block = back[k].astype(F32)
            mixed = block[:, :here].reshape(reps * here, width)
            d_values[k] = block[:, here:].reshape(reps * here, width).astype(BF16)
            d_gate[k] = (grad[k].astype(F32) * mixed).astype(BF16)

        stores[part][0].start()
        stores[part][1].start()
        loads[part][2].wait()
        stores[part][2].start()
    for group in stores:
        for store in group:
            store.wait()


def on_device(grid, grad_out, gate, values, filters, skip):
    reps = lax.axis_size("rep")
    chunks = lax.axis_size("ctx")
    channels, width = values.shape[1:]
    hbm = pl.BlockSpec(memory_space=pl.ANY)
    grad_out, gate, values = (a.reshape(chunks, channels // chunks, width) for a in (grad_out, gate, values))
    consts = [jnp.asarray(t) for t in tables(chunks, width)]
    rows = chunks * 16
    blocks = (reps, chunks, 16, width)
    blocks_back = (chunks, reps, 16, width)
    back, d_filter = pl.pallas_call(
        functools.partial(whole_kernel, reps, chunks, width, grid),
        out_shape=[
            jax.ShapeDtypeStruct(blocks_back, BF16),
            jax.ShapeDtypeStruct(filters.shape, F32),
        ],
        in_specs=[hbm] * (5 + len(consts)),
        out_specs=[hbm] * 2,
        scratch_shapes=[
            pltpu.SMEM(skip.shape, F32),
            pltpu.VMEM(values.shape, BF16),
            pltpu.VMEM(values.shape, BF16),
            pltpu.VMEM(values.shape, BF16),
            pltpu.VMEM((8, filters.shape[1]), F32),
            *(pltpu.VMEM(c.shape, c.dtype) for c in consts),
            pltpu.VMEM((8, filters.shape[1]), F32),
            pltpu.VMEM(blocks_back, BF16),
            pltpu.VMEM(blocks, BF16),
            pltpu.VMEM(blocks, BF16),
            pltpu.VMEM((rows, width), F32),
            pltpu.VMEM((rows, width), F32),
            pltpu.VMEM((chunks * 8, width), F32),
            pltpu.VMEM((8, chunks, 2 * width), F32),
            pltpu.VMEM((8, chunks, 2 * width), F32),
            pltpu.VMEM((8, 2 * chunks, 6 * width), BF16),
            pltpu.VMEM((8, 2 * chunks, 6 * width), BF16),
            pltpu.VMEM((8, width), F32),
            pltpu.VMEM((reps * grid[1], 8, width), F32),
            pltpu.SemaphoreType.DMA((5 + len(consts),)),
            pltpu.SemaphoreType.DMA,
            pltpu.SemaphoreType.DMA,
            pltpu.SemaphoreType.DMA((reps,)),
            pltpu.SemaphoreType.DMA,
            pltpu.SemaphoreType.DMA((reps,)),
            pltpu.SemaphoreType.DMA((reps,)),
            pltpu.SemaphoreType.DMA((reps,)),
            pltpu.SemaphoreType.DMA,
            pltpu.SemaphoreType.DMA((reps * grid[1],)),
        ],
        compiler_params=pltpu.CompilerParams(
            vmem_limit_bytes=56 * 1024 * 1024, collective_id=0, has_side_effects=True
        ),
        name="whole",
    )(skip, grad_out, gate, values, filters, *consts)
    parts = 4
    d_values, d_gate, d_filter = pl.pallas_call(
        functools.partial(finish_kernel, parts),
        out_shape=[
            jax.ShapeDtypeStruct(values.shape, BF16),
            jax.ShapeDtypeStruct(values.shape, BF16),
            jax.ShapeDtypeStruct(filters.shape, F32),
        ],
        in_specs=[hbm] * 3,
        out_specs=[hbm] * 3,
        scratch_shapes=[
            pltpu.VMEM(blocks_back, BF16),
            pltpu.VMEM(values.shape, BF16),
            pltpu.VMEM(filters.shape, F32),
            pltpu.VMEM(values.shape, BF16),
            pltpu.VMEM(values.shape, BF16),
            pltpu.SemaphoreType.DMA((3, parts)),
            pltpu.SemaphoreType.DMA((3, parts)),
        ],
        compiler_params=pltpu.CompilerParams(vmem_limit_bytes=56 * 1024 * 1024),
        name="finish",
    )(back, grad_out, d_filter)
    return d_values.reshape(1, channels, width), d_gate.reshape(1, channels, width), d_filter


def solution(mesh):
    placed = (
        P("rep", None, "ctx"),
        P("rep", None, "ctx"),
        P("rep", None, "ctx"),
        P("ctx", None),
        P("ctx"),
    )
    grid = (mesh.shape["ctx"] // 8, 4, 2)
    return jax.shard_map(
        functools.partial(on_device, grid),
        mesh=mesh,
        in_specs=placed,
        out_specs=(P("rep", None, "ctx"), P("rep", None, "ctx"), P("ctx", None)),
        check_vma=False,
    )
```

```python
import functools
import math

import jax
import jax.numpy as jnp
import ml_dtypes
import numpy as np
from jax import lax
from jax.experimental import pallas as pl
from jax.experimental.pallas import tpu as pltpu
from jax.sharding import PartitionSpec as P

MESH = pl.DeviceIdType.MESH
F32 = jnp.float32
BF16 = jnp.bfloat16


def split_np(table):
    high = table.astype(ml_dtypes.bfloat16)
    low = (table - high.astype(np.float64)).astype(ml_dtypes.bfloat16)
    return high, low


@functools.lru_cache(None)
def tables(chunks, width):
    total = chunks * width
    n = np.arange(chunks)
    q = np.arange(width)
    outer = 2 * np.pi * np.outer(n + 0.25, n) / chunks
    turn = 2 * np.pi * np.outer(n + 0.25, q) / total
    inner = 2 * np.pi * (np.outer(q, q) % width) / width
    first = np.concatenate([np.cos(outer), -np.sin(outer)], axis=0)
    first_hi, first_lo = split_np(first)
    fwd_first = np.concatenate([first_hi, first_lo], axis=1)
    filter_first = np.concatenate([first_hi, first_hi, first_lo], axis=1)
    cos, sin = np.cos(inner), np.sin(inner)
    second = np.block([[cos, -sin], [sin, cos]])
    second_hi, second_lo = split_np(second)
    back_hi, back_lo = split_np(second.T)
    second = np.concatenate([second_hi, second_hi, second_lo], axis=0)
    back = np.concatenate([back_hi, back_hi, back_lo], axis=0)
    last = np.concatenate([np.cos(outer).T, -np.sin(outer).T], axis=1)
    last_hi, last_lo = split_np(last)
    zero = np.zeros_like(last_lo)
    inv_last = np.concatenate(
        [np.concatenate([last_hi, last_hi], axis=1), np.concatenate([last_lo, zero], axis=1)], axis=0
    )
    twist = np.stack([np.cos(turn), np.sin(turn)]).astype(np.float32)
    return fwd_first, filter_first, second, back, inv_last, twist


def dot(left, right):
    return jnp.dot(left, right, preferred_element_type=F32)


def split(array):
    high = array.astype(BF16)
    low = (array - high.astype(F32)).astype(BF16)
    return high, low


def split3(array):
    high, low = split(array)
    return jnp.concatenate([high, low, high], axis=1)


def whole_kernel(
    reps, chunks, width, grid,
    skip_hbm, grad_hbm, gate_hbm, value_hbm, filter_hbm,
    first_hbm, filter_first_hbm, second_hbm, back_hbm, last_hbm, twist_hbm,
    back, d_filter_hbm,
    skip_ref, grad_ref, gate_ref, value_ref, filter_ref,
    first_ref, filter_first_ref, second_ref, back_ref, last_ref, twist_ref,
    d_filter_ref,
    send, recv, result_out, rows_in, rows_out, filter_rows, filter_spec, cross, spectra, products, note_out, note_in,
    in_sem, own_sem,
    send_sem, recv_sem, back_send_sem, back_sem, filter_send_sem, filter_sem, note_send_sem, note_sem,
):
    here = 8
    nz, ny, nx = grid
    rep = lax.axis_index("rep")
    ctx = lax.axis_index("ctx")
    z, y, x = lax.div(ctx, ny * nx), lax.rem(lax.div(ctx, nx), ny), lax.rem(ctx, nx)
    mine = rep * here
    scale = 1.0 / (chunks * width)

    swing_z = [0] + [d * sign for d in range(1, nz // 2) for sign in (1, -1)] + [nz // 2]
    to_z = [lax.rem(z + step + nz, nz) * (ny * nx) for step in swing_z]

    def to_yx(turn_y, turn_x):
        return lax.rem(y + turn_y, ny) * nx + lax.rem(x + turn_x, nx)

    stay = to_yx(0, 0)

    def around(start, stop, act):
        @pl.loop(start, stop)
        def _(step):
            phase, rest = lax.div(step, ny * nx), lax.rem(step, ny * nx)
            turn_x = lax.rem(rest, nx)
            there = to_yx(lax.div(rest, nx), turn_x)
            act(phase, turn_x, there)

    tiers = ((0, 1), (1, nz))

    def early_first(act):
        for low, high in tiers:
            @pl.loop(0, ny * nx)
            def _(rest):
                there = to_yx(lax.div(rest, nx), lax.rem(rest, nx))
                if high == low + 1:
                    act(low * (ny * nx) + there)
                else:
                    for start in to_z:
                        @pl.when((start >= low * (ny * nx)) & (start < high * (ny * nx)))
                        def _():
                            act(start + there)

    def along_row(act):
        for n, start in enumerate(to_z):
            for turn_x in range(nx):
                if n or turn_x:
                    act(0, start + to_yx(0, turn_x))

    def along_column(act):
        for phase in range(reps):
            for turn_y in range(ny):
                if phase or turn_y:
                    act(phase, to_z[0] + to_yx(turn_y, 0))

    def peer(phase):
        base = lax.rem(rep + lax.div(phase, 2) * 2, reps)
        return base + lax.rem(phase, 2) * (1 - lax.rem(base, 2) * 2)

    def twisted(section):
        cos, sin = twist_ref[0], twist_ref[1]
        real, imag = section[:chunks], section[chunks:]
        return jnp.concatenate([real * cos + imag * sin, imag * cos - real * sin], axis=1)

    def untwisted(section):
        cos, sin = twist_ref[0], twist_ref[1]
        real, imag = section[:, :width], section[:, width:]
        return jnp.concatenate([real * cos - imag * sin, imag * cos + real * sin], axis=0)

    own = pl.ds(pl.multiple_of(mine, here), here)
    loads = [
        pltpu.make_async_copy(src, dst, in_sem.at[n])
        for n, (src, dst) in enumerate((
            (grad_hbm, grad_ref), (gate_hbm, gate_ref), (value_hbm, value_ref),
            (filter_hbm.at[own], filter_ref), (filter_first_hbm, filter_first_ref), (twist_hbm, twist_ref),
            (second_hbm, second_ref), (first_hbm, first_ref),
            (back_hbm, back_ref), (last_hbm, last_ref), (skip_hbm, skip_ref),
        ))
    ]
    for load in loads:
        load.start()

    barrier = pltpu.get_barrier_semaphore()

    def greet(phase, j):
        pl.semaphore_signal(barrier, 1, device_id=(peer(phase), j), device_id_type=MESH)

    along_row(greet)
    along_column(greet)

    for load in loads[:3]:
        load.wait()

    @pl.loop(0, chunks, unroll=4)
    def _(j):
        value = value_ref[j].astype(F32)
        d_conv = grad_ref[j].astype(F32) * gate_ref[j].astype(F32)
        both = jnp.concatenate([value.reshape(reps, here, width), d_conv.reshape(reps, here, width)], axis=1)
        send[j] = both.astype(BF16)

    note_out[...] = jnp.zeros_like(note_out)
    pltpu.make_async_copy(send.at[ctx, rep], recv.at[0, ctx], recv_sem.at[0]).start()
    pl.semaphore_wait(barrier, nz * nx + reps * ny - 2)

    def note(phase, j):
        pltpu.make_async_remote_copy(
            src_ref=note_out, dst_ref=note_in.at[rep * ny + y],
            send_sem=note_send_sem, recv_sem=note_sem.at[rep * ny + y],
            device_id=(peer(phase), j), device_id_type=MESH,
        ).start()

    def send_block(phase, j):
        i = peer(phase)
        pltpu.make_async_remote_copy(
            src_ref=send.at[j, i], dst_ref=recv.at[phase, ctx],
            send_sem=send_sem, recv_sem=recv_sem.at[phase], device_id=(i, j), device_id_type=MESH,
        ).start()

    along_column(note)
    along_row(send_block)
    along_column(send_block)

    @pl.loop(1, reps * ny)
    def _(step):
        there = lax.rem(step, ny)
        sender = peer(lax.div(step, ny)) * ny + lax.rem(y + there, ny)
        pltpu.make_async_copy(note_in.at[sender], note_in.at[sender], note_sem.at[sender]).wait()
        for turn_x in range(nx):
            for start in to_z[0 if turn_x else 1:]:
                send_block(lax.div(step, ny), start + to_yx(there, turn_x))


    for load in loads[3:]:
        load.wait()

    for n in range(chunks):
        filter_rows[n * here:(n + 1) * here, :] = filter_ref[:, n * width:(n + 1) * width]

    def last_step(both):
        high, low = split(both)
        parts = dot(last_ref[...], jnp.concatenate([high, low], axis=0))
        return parts[:chunks] + parts[chunks:]

    @pl.loop(0, here, unroll=4)
    def _(c):
        high, low = split(filter_rows[pl.ds(c, chunks, stride=here), :])
        section = dot(filter_first_ref[...], jnp.concatenate([high, low, high], axis=0))
        filter_spec[c] = dot(split3(twisted(section)), second_ref[...]) * scale
        cross[c] = jnp.zeros((chunks, 2 * width), F32)

    def to_spectra(phase):
        rows_in[:chunks * 16] = recv[phase].astype(F32).reshape(chunks * 16, width)

        @pl.loop(0, here, unroll=here)
        def _(c):
            value = rows_in[pl.ds(c, chunks, stride=16), :].astype(BF16)
            d_conv = rows_in[pl.ds(c + here, chunks, stride=16), :].astype(BF16)
            pair = jnp.concatenate([value, d_conv], axis=1)
            section = dot(first_ref[...], jnp.concatenate([pair, pair], axis=0))
            spectra[c, :chunks] = split3(twisted(section[:, :width]))
            spectra[c, chunks:] = split3(twisted(section[:, width:]))

        full = dot(spectra[...].reshape(here * 2 * chunks, 6 * width), second_ref[...])
        full = full.reshape(here, 2 * chunks, 2 * width)
        for c in range(here):
            vr, vi = full[c, :chunks, :width], full[c, :chunks, width:]
            dr, di = full[c, chunks:, :width], full[c, chunks:, width:]
            fr, fi = filter_spec[c, :, :width], filter_spec[c, :, width:]
            cross[c, :, :width] += dr * vr + di * vi
            cross[c, :, width:] += di * vr - dr * vi
            products[c, :chunks] = split3(jnp.concatenate([fr * vr - fi * vi, fr * vi + fi * vr], axis=1))
            products[c, chunks:] = split3(jnp.concatenate([fr * dr + fi * di, fr * di - fi * dr], axis=1))

    def from_products(phase):
        full = dot(products[...].reshape(here * 2 * chunks, 6 * width), back_ref[...])
        full = full.reshape(here, 2 * chunks, 2 * width)
        for c in range(here):
            skip = skip_ref[mine + c]
            result = last_step(jnp.concatenate([untwisted(full[c, :chunks]), untwisted(full[c, chunks:])], axis=1))
            value = rows_in[pl.ds(c, chunks, stride=16), :]
            d_conv = rows_in[pl.ds(c + here, chunks, stride=16), :]
            rows_out[pl.ds(c, chunks, stride=16), :] = result[:, :width] + skip * value
            rows_out[pl.ds(c + here, chunks, stride=16), :] = result[:, width:] + skip * d_conv
        result_out[phase] = rows_out[:chunks * 16].reshape(chunks, 16, width).astype(BF16)

    def send_back(phase, j):
        pltpu.make_async_remote_copy(
            src_ref=result_out.at[phase, j], dst_ref=back.at[ctx, rep],
            send_sem=back_send_sem, recv_sem=back_sem.at[phase], device_id=(peer(phase), j), device_id_type=MESH,
        ).start()

    def send_back_ring(phase, turn_x, there):
        @pl.when((phase > 0) | (there != stay))
        def _():
            send_back(phase, to_z[0] + there)

        for start in to_z[1:]:
            send_back(phase, start + there)

    def wait_blocks(phase, sem):
        pltpu.make_async_copy(recv.at[phase], recv.at[phase], sem.at[phase]).wait()

    factor = scale / math.sqrt(reps * chunks * width)
    sibling = (peer(1), ctx)

    def filter_copy(n, src, phase, device):
        block = pl.ds(pl.multiple_of(peer(phase) * here, here), here)
        return pltpu.make_async_remote_copy(
            src_ref=src if phase == 0 else src.at[block], dst_ref=d_filter_hbm.at[block],
            send_sem=filter_send_sem.at[n], recv_sem=filter_sem.at[n], device_id=device, device_id_type=MESH,
        )

    to_sibling = filter_copy(0, d_filter_ref, 0, sibling)
    across = filter_copy(1, d_filter_ref, 0, (peer(2), ctx))
    onward = filter_copy(2, d_filter_hbm, 2, sibling)
    own_store = pltpu.make_async_copy(d_filter_ref, d_filter_hbm.at[own], own_sem)

    @pl.loop(0, reps)
    def _(phase):
        wait_blocks(phase, recv_sem)
        to_spectra(phase)

        @pl.when(phase == reps - 1)
        def _():
            @pl.loop(0, here // 2, unroll=4)
            def _(g):
                both = [untwisted(dot(split3(cross[2 * g + e] * factor), back_ref[...])) for e in range(2)]
                result = last_step(jnp.concatenate(both, axis=1))
                for e in range(2):
                    filter_rows[pl.ds(2 * g + e, chunks, stride=here), :] = result[:, e * width:(e + 1) * width]

            for n in range(chunks):
                d_filter_ref[:, n * width:(n + 1) * width] = filter_rows[n * here:(n + 1) * here, :]
            across.start()
            to_sibling.start()
            own_store.start()

        from_products(phase)

        @pl.when(phase == 0)
        def _():
            pltpu.make_async_copy(result_out.at[0, ctx], back.at[ctx, rep], back_sem.at[0]).start()

        @pl.when(phase < reps - 1)
        def _():
            around(phase * (ny * nx), (phase + 1) * (ny * nx), send_back_ring)

        @pl.when(phase == reps - 1)
        def _():
            early_first(lambda j: send_back(reps - 1, j))

    for phase in range(reps // 2):
        wait_blocks(phase, back_sem)
    across.wait_recv()
    onward.start()
    for phase in range(reps // 2, reps):
        wait_blocks(phase, back_sem)
    to_sibling.wait_recv()
    onward.wait_recv()
    own_store.wait()
    for copy in (to_sibling, across, onward):
        copy.wait_send()
    notes = note_in.at[pl.ds(0, reps * ny - 1)]
    pltpu.make_async_copy(notes, notes, note_send_sem).wait()
    sent = send.at[pl.ds(0, chunks - 1)]
    rest = send.at[chunks - 1, pl.ds(0, reps - 1)]
    for sem in (send_sem, back_send_sem):
        pltpu.make_async_copy(sent, sent, sem).wait()
        pltpu.make_async_copy(rest, rest, sem).wait()


def finish_kernel(
    parts, back_hbm, grad_hbm, filter_hbm, d_values_hbm, d_gate_hbm, d_filter_hbm,
    back, grad, kept, d_values, d_gate, in_sem, out_sem,
):
    chunks, reps, rows, width = back.shape
    here = rows // 2
    size, kept_size = chunks // parts, kept.shape[0] // parts
    loads, stores = [], []
    for part in range(parts):
        cut, kept_cut = pl.ds(part * size, size), pl.ds(part * kept_size, kept_size)
        loads.append([
            pltpu.make_async_copy(src.at[c], dst.at[c], in_sem.at[n, part])
            for n, (src, dst, c) in enumerate(((back_hbm, back, cut), (grad_hbm, grad, cut), (filter_hbm, kept, kept_cut)))
        ])
        stores.append([
            pltpu.make_async_copy(src.at[c], dst.at[c], out_sem.at[n, part])
            for n, (src, dst, c) in enumerate((
                (d_values, d_values_hbm, cut), (d_gate, d_gate_hbm, cut), (kept, d_filter_hbm, kept_cut)
            ))
        ])
        for load in loads[-1]:
            load.start()
    for part in range(parts):
        loads[part][0].wait()
        loads[part][1].wait()

        @pl.loop(part * size, (part + 1) * size, unroll=4)
        def _(k):
            block = back[k].astype(F32)
            mixed = block[:, :here].reshape(reps * here, width)
            d_values[k] = block[:, here:].reshape(reps * here, width).astype(BF16)
            d_gate[k] = (grad[k].astype(F32) * mixed).astype(BF16)

        stores[part][0].start()
        stores[part][1].start()
        loads[part][2].wait()
        stores[part][2].start()
    for group in stores:
        for store in group:
            store.wait()


def on_device(grid, grad_out, gate, values, filters, skip):
    reps = lax.axis_size("rep")
    chunks = lax.axis_size("ctx")
    channels, width = values.shape[1:]
    hbm = pl.BlockSpec(memory_space=pl.ANY)
    grad_out, gate, values = (a.reshape(chunks, channels // chunks, width) for a in (grad_out, gate, values))
    consts = [jnp.asarray(t) for t in tables(chunks, width)]
    rows = chunks * 16
    blocks = (reps, chunks, 16, width)
    blocks_back = (chunks, reps, 16, width)
    back, d_filter = pl.pallas_call(
        functools.partial(whole_kernel, reps, chunks, width, grid),
        out_shape=[
            jax.ShapeDtypeStruct(blocks_back, BF16),
            jax.ShapeDtypeStruct(filters.shape, F32),
        ],
        in_specs=[hbm] * (5 + len(consts)),
        out_specs=[hbm] * 2,
        scratch_shapes=[
            pltpu.SMEM(skip.shape, F32),
            pltpu.VMEM(values.shape, BF16),
            pltpu.VMEM(values.shape, BF16),
            pltpu.VMEM(values.shape, BF16),
            pltpu.VMEM((8, filters.shape[1]), F32),
            *(pltpu.VMEM(c.shape, c.dtype) for c in consts),
            pltpu.VMEM((8, filters.shape[1]), F32),
            pltpu.VMEM(blocks_back, BF16),
            pltpu.VMEM(blocks, BF16),
            pltpu.VMEM(blocks, BF16),
            pltpu.VMEM((rows + 16, width), F32),
            pltpu.VMEM((rows + 16, width), F32),
            pltpu.VMEM((chunks * 8 + 8, width), F32),
            pltpu.VMEM((8, chunks, 2 * width), F32),
            pltpu.VMEM((8, chunks, 2 * width), F32),
            pltpu.VMEM((8, 2 * chunks, 6 * width), BF16),
            pltpu.VMEM((8, 2 * chunks, 6 * width), BF16),
            pltpu.VMEM((8, width), F32),
            pltpu.VMEM((reps * grid[1], 8, width), F32),
            pltpu.SemaphoreType.DMA((5 + len(consts),)),
            pltpu.SemaphoreType.DMA,
            pltpu.SemaphoreType.DMA,
            pltpu.SemaphoreType.DMA((reps,)),
            pltpu.SemaphoreType.DMA,
            pltpu.SemaphoreType.DMA((reps,)),
            pltpu.SemaphoreType.DMA((reps,)),
            pltpu.SemaphoreType.DMA((reps,)),
            pltpu.SemaphoreType.DMA,
            pltpu.SemaphoreType.DMA((reps * grid[1],)),
        ],
        compiler_params=pltpu.CompilerParams(
            vmem_limit_bytes=56 * 1024 * 1024, collective_id=0, has_side_effects=True
        ),
        name="whole",
    )(skip, grad_out, gate, values, filters, *consts)
    parts = 4
    d_values, d_gate, d_filter = pl.pallas_call(
        functools.partial(finish_kernel, parts),
        out_shape=[
            jax.ShapeDtypeStruct(values.shape, BF16),
            jax.ShapeDtypeStruct(values.shape, BF16),
            jax.ShapeDtypeStruct(filters.shape, F32),
        ],
        in_specs=[hbm] * 3,
        out_specs=[hbm] * 3,
        scratch_shapes=[
            pltpu.VMEM(blocks_back, BF16),
            pltpu.VMEM(values.shape, BF16),
            pltpu.VMEM(filters.shape, F32),
            pltpu.VMEM(values.shape, BF16),
            pltpu.VMEM(values.shape, BF16),
            pltpu.SemaphoreType.DMA((3, parts)),
            pltpu.SemaphoreType.DMA((3, parts)),
        ],
        compiler_params=pltpu.CompilerParams(vmem_limit_bytes=56 * 1024 * 1024),
        name="finish",
    )(back, grad_out, d_filter)
    return d_values.reshape(1, channels, width), d_gate.reshape(1, channels, width), d_filter


def solution(mesh):
    placed = (
        P("rep", None, "ctx"),
        P("rep", None, "ctx"),
        P("rep", None, "ctx"),
        P("ctx", None),
        P("ctx"),
    )
    grid = (mesh.shape["ctx"] // 8, 4, 2)
    return jax.shard_map(
        functools.partial(on_device, grid),
        mesh=mesh,
        in_specs=placed,
        out_specs=(P("rep", None, "ctx"), P("rep", None, "ctx"), P("ctx", None)),
        check_vma=False,
    )
```

```python
import functools
import math

import jax
import jax.numpy as jnp
import ml_dtypes
import numpy as np
from jax import lax
from jax.experimental import pallas as pl
from jax.experimental.pallas import tpu as pltpu
from jax.sharding import PartitionSpec as P

MESH = pl.DeviceIdType.MESH
F32 = jnp.float32
BF16 = jnp.bfloat16


def split_np(table):
    high = table.astype(ml_dtypes.bfloat16)
    low = (table - high.astype(np.float64)).astype(ml_dtypes.bfloat16)
    return high, low


@functools.lru_cache(None)
def tables(chunks, width):
    total = chunks * width
    n = np.arange(chunks)
    q = np.arange(width)
    outer = 2 * np.pi * np.outer(n + 0.25, n) / chunks
    turn = 2 * np.pi * np.outer(n + 0.25, q) / total
    inner = 2 * np.pi * (np.outer(q, q) % width) / width
    first = np.concatenate([np.cos(outer), -np.sin(outer)], axis=0)
    first_hi, first_lo = split_np(first)
    fwd_first = np.concatenate([first_hi, first_lo], axis=1)
    filter_first = np.concatenate([first_hi, first_hi, first_lo], axis=1)
    cos, sin = np.cos(inner), np.sin(inner)
    second = np.block([[cos, -sin], [sin, cos]])
    second_hi, second_lo = split_np(second)
    back_hi, back_lo = split_np(second.T)
    second = np.concatenate([second_hi, second_hi, second_lo], axis=0)
    back = np.concatenate([back_hi, back_hi, back_lo], axis=0)
    last = np.concatenate([np.cos(outer).T, -np.sin(outer).T], axis=1)
    last_hi, last_lo = split_np(last)
    zero = np.zeros_like(last_lo)
    inv_last = np.concatenate(
        [np.concatenate([last_hi, last_hi], axis=1), np.concatenate([last_lo, zero], axis=1)], axis=0
    )
    twist = np.stack([np.cos(turn), np.sin(turn)]).astype(np.float32)
    return fwd_first, filter_first, second, back, inv_last, twist


def dot(left, right):
    return jnp.dot(left, right, preferred_element_type=F32)


def split(array):
    high = array.astype(BF16)
    low = (array - high.astype(F32)).astype(BF16)
    return high, low


def split3(array):
    high, low = split(array)
    return jnp.concatenate([high, low, high], axis=1)


def whole_kernel(
    reps, chunks, width, grid,
    skip_hbm, grad_hbm, gate_hbm, value_hbm, filter_hbm,
    first_hbm, filter_first_hbm, second_hbm, back_hbm, last_hbm, twist_hbm,
    back, d_filter_hbm,
    skip_ref, grad_ref, gate_ref, value_ref, filter_ref,
    first_ref, filter_first_ref, second_ref, back_ref, last_ref, twist_ref,
    d_filter_ref,
    send, recv, result_out, rows_in, rows_out, filter_rows, filter_spec, cross, spectra, products, note_out, note_in,
    in_sem, own_sem,
    send_sem, recv_sem, back_send_sem, back_sem, filter_send_sem, filter_sem, note_send_sem, note_sem,
):
    here = 8
    nz, ny, nx = grid
    rep = lax.axis_index("rep")
    ctx = lax.axis_index("ctx")
    z, y, x = lax.div(ctx, ny * nx), lax.rem(lax.div(ctx, nx), ny), lax.rem(ctx, nx)
    mine = rep * here
    scale = 1.0 / (chunks * width)

    swing_z = [0] + [d * sign for d in range(1, nz // 2) for sign in (1, -1)] + [nz // 2]
    to_z = [lax.rem(z + step + nz, nz) * (ny * nx) for step in swing_z]

    def to_yx(turn_y, turn_x):
        return lax.rem(y + turn_y, ny) * nx + lax.rem(x + turn_x, nx)

    tiers = ((0, 1), (1, nz))

    def early_first(act):
        for low, high in tiers:
            @pl.loop(0, ny * nx)
            def _(rest):
                there = to_yx(lax.div(rest, nx), lax.rem(rest, nx))
                if high == low + 1:
                    act(low * (ny * nx) + there)
                else:
                    for start in to_z:
                        @pl.when((start >= low * (ny * nx)) & (start < high * (ny * nx)))
                        def _():
                            act(start + there)

    def along_row(act):
        for n, start in enumerate(to_z):
            for turn_x in range(nx):
                if n or turn_x:
                    act(0, start + to_yx(0, turn_x))

    def along_column(act):
        for phase in range(reps):
            for turn_y in range(ny):
                if phase or turn_y:
                    act(phase, to_z[0] + to_yx(turn_y, 0))

    def peer(phase):
        base = lax.rem(rep + lax.div(phase, 2) * 2, reps)
        return base + lax.rem(phase, 2) * (1 - lax.rem(base, 2) * 2)

    def twisted(section):
        cos, sin = twist_ref[0], twist_ref[1]
        real, imag = section[:chunks], section[chunks:]
        return jnp.concatenate([real * cos + imag * sin, imag * cos - real * sin], axis=1)

    def untwisted(section):
        cos, sin = twist_ref[0], twist_ref[1]
        real, imag = section[:, :width], section[:, width:]
        return jnp.concatenate([real * cos - imag * sin, imag * cos + real * sin], axis=0)

    own = pl.ds(pl.multiple_of(mine, here), here)
    loads = [
        pltpu.make_async_copy(src, dst, in_sem.at[n])
        for n, (src, dst) in enumerate((
            (grad_hbm, grad_ref), (gate_hbm, gate_ref), (value_hbm, value_ref),
            (filter_hbm.at[own], filter_ref), (filter_first_hbm, filter_first_ref), (twist_hbm, twist_ref),
            (second_hbm, second_ref), (first_hbm, first_ref),
            (back_hbm, back_ref), (last_hbm, last_ref), (skip_hbm, skip_ref),
        ))
    ]
    for load in loads:
        load.start()

    barrier = pltpu.get_barrier_semaphore()

    def greet(phase, j):
        pl.semaphore_signal(barrier, 1, device_id=(peer(phase), j), device_id_type=MESH)

    along_row(greet)
    along_column(greet)

    for load in loads[:3]:
        load.wait()

    @pl.loop(0, chunks, unroll=4)
    def _(j):
        value = value_ref[j].astype(F32)
        d_conv = grad_ref[j].astype(F32) * gate_ref[j].astype(F32)
        both = jnp.concatenate([value.reshape(reps, here, width), d_conv.reshape(reps, here, width)], axis=1)
        send[j] = both.astype(BF16)

    note_out[...] = jnp.zeros_like(note_out)
    pltpu.make_async_copy(send.at[ctx, rep], recv.at[0, ctx], recv_sem.at[0]).start()
    pl.semaphore_wait(barrier, nz * nx + reps * ny - 2)

    def note(phase, j):
        pltpu.make_async_remote_copy(
            src_ref=note_out, dst_ref=note_in.at[rep * ny + y],
            send_sem=note_send_sem, recv_sem=note_sem.at[rep * ny + y],
            device_id=(peer(phase), j), device_id_type=MESH,
        ).start()

    def send_block(phase, j):
        i = peer(phase)
        pltpu.make_async_remote_copy(
            src_ref=send.at[j, i], dst_ref=recv.at[phase, ctx],
            send_sem=send_sem, recv_sem=recv_sem.at[phase], device_id=(i, j), device_id_type=MESH,
        ).start()

    along_column(note)
    along_row(send_block)
    along_column(send_block)

    @pl.loop(1, reps * ny)
    def _(step):
        there = lax.rem(step, ny)
        sender = peer(lax.div(step, ny)) * ny + lax.rem(y + there, ny)
        pltpu.make_async_copy(note_in.at[sender], note_in.at[sender], note_sem.at[sender]).wait()
        for turn_x in range(nx):
            for start in to_z[0 if turn_x else 1:]:
                send_block(lax.div(step, ny), start + to_yx(there, turn_x))


    for load in loads[3:]:
        load.wait()

    for n in range(chunks):
        filter_rows[n * here:(n + 1) * here, :] = filter_ref[:, n * width:(n + 1) * width]

    def last_step(both):
        high, low = split(both)
        parts = dot(last_ref[...], jnp.concatenate([high, low], axis=0))
        return parts[:chunks] + parts[chunks:]

    @pl.loop(0, here, unroll=4)
    def _(c):
        high, low = split(filter_rows[pl.ds(c, chunks, stride=here), :])
        section = dot(filter_first_ref[...], jnp.concatenate([high, low, high], axis=0))
        filter_spec[c] = dot(split3(twisted(section)), second_ref[...]) * scale
        cross[c] = jnp.zeros((chunks, 2 * width), F32)

    def to_spectra(phase):
        rows_in[:chunks * 16] = recv[phase].astype(F32).reshape(chunks * 16, width)

        @pl.loop(0, here, unroll=here)
        def _(c):
            value = rows_in[pl.ds(c, chunks, stride=16), :].astype(BF16)
            d_conv = rows_in[pl.ds(c + here, chunks, stride=16), :].astype(BF16)
            pair = jnp.concatenate([value, d_conv], axis=1)
            section = dot(first_ref[...], jnp.concatenate([pair, pair], axis=0))
            spectra[c, :chunks] = split3(twisted(section[:, :width]))
            spectra[c, chunks:] = split3(twisted(section[:, width:]))

        full = dot(spectra[...].reshape(here * 2 * chunks, 6 * width), second_ref[...])
        full = full.reshape(here, 2 * chunks, 2 * width)
        for c in range(here):
            vr, vi = full[c, :chunks, :width], full[c, :chunks, width:]
            dr, di = full[c, chunks:, :width], full[c, chunks:, width:]
            fr, fi = filter_spec[c, :, :width], filter_spec[c, :, width:]
            cross[c, :, :width] += dr * vr + di * vi
            cross[c, :, width:] += di * vr - dr * vi
            products[c, :chunks] = split3(jnp.concatenate([fr * vr - fi * vi, fr * vi + fi * vr], axis=1))
            products[c, chunks:] = split3(jnp.concatenate([fr * dr + fi * di, fr * di - fi * dr], axis=1))

    def from_products(phase):
        full = dot(products[...].reshape(here * 2 * chunks, 6 * width), back_ref[...])
        full = full.reshape(here, 2 * chunks, 2 * width)
        for c in range(here):
            skip = skip_ref[mine + c]
            result = last_step(jnp.concatenate([untwisted(full[c, :chunks]), untwisted(full[c, chunks:])], axis=1))
            value = rows_in[pl.ds(c, chunks, stride=16), :]
            d_conv = rows_in[pl.ds(c + here, chunks, stride=16), :]
            rows_out[pl.ds(c, chunks, stride=16), :] = result[:, :width] + skip * value
            rows_out[pl.ds(c + here, chunks, stride=16), :] = result[:, width:] + skip * d_conv
        result_out[phase] = rows_out[:chunks * 16].reshape(chunks, 16, width).astype(BF16)

    def send_back(phase, j):
        pltpu.make_async_remote_copy(
            src_ref=result_out.at[phase, j], dst_ref=back.at[ctx, rep],
            send_sem=back_send_sem, recv_sem=back_sem.at[phase], device_id=(peer(phase), j), device_id_type=MESH,
        ).start()

    def wait_blocks(phase, sem):
        pltpu.make_async_copy(recv.at[phase], recv.at[phase], sem.at[phase]).wait()

    factor = scale / math.sqrt(reps * chunks * width)
    sibling = (peer(1), ctx)

    def filter_copy(n, src, phase, device):
        block = pl.ds(pl.multiple_of(peer(phase) * here, here), here)
        return pltpu.make_async_remote_copy(
            src_ref=src if phase == 0 else src.at[block], dst_ref=d_filter_hbm.at[block],
            send_sem=filter_send_sem.at[n], recv_sem=filter_sem.at[n], device_id=device, device_id_type=MESH,
        )

    to_sibling = filter_copy(0, d_filter_ref, 0, sibling)
    across = filter_copy(1, d_filter_ref, 0, (peer(2), ctx))
    onward = filter_copy(2, d_filter_hbm, 2, sibling)
    own_store = pltpu.make_async_copy(d_filter_ref, d_filter_hbm.at[own], own_sem)

    @pl.loop(0, reps)
    def _(phase):
        wait_blocks(phase, recv_sem)
        to_spectra(phase)

        @pl.when(phase == reps - 1)
        def _():
            @pl.loop(0, here // 2, unroll=4)
            def _(g):
                both = [untwisted(dot(split3(cross[2 * g + e] * factor), back_ref[...])) for e in range(2)]
                result = last_step(jnp.concatenate(both, axis=1))
                for e in range(2):
                    filter_rows[pl.ds(2 * g + e, chunks, stride=here), :] = result[:, e * width:(e + 1) * width]

            for n in range(chunks):
                d_filter_ref[:, n * width:(n + 1) * width] = filter_rows[n * here:(n + 1) * here, :]
            across.start()
            to_sibling.start()
            own_store.start()

        from_products(phase)

        @pl.when(phase == 0)
        def _():
            pltpu.make_async_copy(result_out.at[0, ctx], back.at[ctx, rep], back_sem.at[0]).start()

        def send_result(j):
            @pl.when((phase > 0) | (j != ctx))
            def _():
                send_back(phase, j)

        early_first(send_result)

    for phase in range(reps // 2):
        wait_blocks(phase, back_sem)
    across.wait_recv()
    onward.start()
    for phase in range(reps // 2, reps):
        wait_blocks(phase, back_sem)
    to_sibling.wait_recv()
    onward.wait_recv()
    own_store.wait()
    for copy in (to_sibling, across, onward):
        copy.wait_send()
    notes = note_in.at[pl.ds(0, reps * ny - 1)]
    pltpu.make_async_copy(notes, notes, note_send_sem).wait()
    sent = send.at[pl.ds(0, chunks - 1)]
    rest = send.at[chunks - 1, pl.ds(0, reps - 1)]
    for sem in (send_sem, back_send_sem):
        pltpu.make_async_copy(sent, sent, sem).wait()
        pltpu.make_async_copy(rest, rest, sem).wait()


def finish_kernel(
    parts, back_hbm, grad_hbm, filter_hbm, d_values_hbm, d_gate_hbm, d_filter_hbm,
    back, grad, kept, d_values, d_gate, in_sem, out_sem,
):
    chunks, reps, rows, width = back.shape
    here = rows // 2
    size, kept_size = chunks // parts, kept.shape[0] // parts
    loads, stores = [], []
    for part in range(parts):
        cut, kept_cut = pl.ds(part * size, size), pl.ds(part * kept_size, kept_size)
        loads.append([
            pltpu.make_async_copy(src.at[c], dst.at[c], in_sem.at[n, part])
            for n, (src, dst, c) in enumerate(((back_hbm, back, cut), (grad_hbm, grad, cut), (filter_hbm, kept, kept_cut)))
        ])
        stores.append([
            pltpu.make_async_copy(src.at[c], dst.at[c], out_sem.at[n, part])
            for n, (src, dst, c) in enumerate((
                (d_values, d_values_hbm, cut), (d_gate, d_gate_hbm, cut), (kept, d_filter_hbm, kept_cut)
            ))
        ])
        for load in loads[-1]:
            load.start()
    for part in range(parts):
        loads[part][0].wait()
        loads[part][1].wait()

        @pl.loop(part * size, (part + 1) * size, unroll=4)
        def _(k):
            block = back[k].astype(F32)
            mixed = block[:, :here].reshape(reps * here, width)
            d_values[k] = block[:, here:].reshape(reps * here, width).astype(BF16)
            d_gate[k] = (grad[k].astype(F32) * mixed).astype(BF16)

        stores[part][0].start()
        stores[part][1].start()
        loads[part][2].wait()
        stores[part][2].start()
    for group in stores:
        for store in group:
            store.wait()


def on_device(grid, grad_out, gate, values, filters, skip):
    reps = lax.axis_size("rep")
    chunks = lax.axis_size("ctx")
    channels, width = values.shape[1:]
    hbm = pl.BlockSpec(memory_space=pl.ANY)
    grad_out, gate, values = (a.reshape(chunks, channels // chunks, width) for a in (grad_out, gate, values))
    consts = [jnp.asarray(t) for t in tables(chunks, width)]
    rows = chunks * 16
    blocks = (reps, chunks, 16, width)
    blocks_back = (chunks, reps, 16, width)
    back, d_filter = pl.pallas_call(
        functools.partial(whole_kernel, reps, chunks, width, grid),
        out_shape=[
            jax.ShapeDtypeStruct(blocks_back, BF16),
            jax.ShapeDtypeStruct(filters.shape, F32),
        ],
        in_specs=[hbm] * (5 + len(consts)),
        out_specs=[hbm] * 2,
        scratch_shapes=[
            pltpu.SMEM(skip.shape, F32),
            pltpu.VMEM(values.shape, BF16),
            pltpu.VMEM(values.shape, BF16),
            pltpu.VMEM(values.shape, BF16),
            pltpu.VMEM((8, filters.shape[1]), F32),
            *(pltpu.VMEM(c.shape, c.dtype) for c in consts),
            pltpu.VMEM((8, filters.shape[1]), F32),
            pltpu.VMEM(blocks_back, BF16),
            pltpu.VMEM(blocks, BF16),
            pltpu.VMEM(blocks, BF16),
            pltpu.VMEM((rows + 16, width), F32),
            pltpu.VMEM((rows + 16, width), F32),
            pltpu.VMEM((chunks * 8 + 8, width), F32),
            pltpu.VMEM((8, chunks, 2 * width), F32),
            pltpu.VMEM((8, chunks, 2 * width), F32),
            pltpu.VMEM((8, 2 * chunks, 6 * width), BF16),
            pltpu.VMEM((8, 2 * chunks, 6 * width), BF16),
            pltpu.VMEM((8, width), F32),
            pltpu.VMEM((reps * grid[1], 8, width), F32),
            pltpu.SemaphoreType.DMA((5 + len(consts),)),
            pltpu.SemaphoreType.DMA,
            pltpu.SemaphoreType.DMA,
            pltpu.SemaphoreType.DMA((reps,)),
            pltpu.SemaphoreType.DMA,
            pltpu.SemaphoreType.DMA((reps,)),
            pltpu.SemaphoreType.DMA((reps,)),
            pltpu.SemaphoreType.DMA((reps,)),
            pltpu.SemaphoreType.DMA,
            pltpu.SemaphoreType.DMA((reps * grid[1],)),
        ],
        compiler_params=pltpu.CompilerParams(
            vmem_limit_bytes=56 * 1024 * 1024, collective_id=0, has_side_effects=True
        ),
        name="whole",
    )(skip, grad_out, gate, values, filters, *consts)
    parts = 4
    d_values, d_gate, d_filter = pl.pallas_call(
        functools.partial(finish_kernel, parts),
        out_shape=[
            jax.ShapeDtypeStruct(values.shape, BF16),
            jax.ShapeDtypeStruct(values.shape, BF16),
            jax.ShapeDtypeStruct(filters.shape, F32),
        ],
        in_specs=[hbm] * 3,
        out_specs=[hbm] * 3,
        scratch_shapes=[
            pltpu.VMEM(blocks_back, BF16),
            pltpu.VMEM(values.shape, BF16),
            pltpu.VMEM(filters.shape, F32),
            pltpu.VMEM(values.shape, BF16),
            pltpu.VMEM(values.shape, BF16),
            pltpu.SemaphoreType.DMA((3, parts)),
            pltpu.SemaphoreType.DMA((3, parts)),
        ],
        compiler_params=pltpu.CompilerParams(vmem_limit_bytes=56 * 1024 * 1024),
        name="finish",
    )(back, grad_out, d_filter)
    return d_values.reshape(1, channels, width), d_gate.reshape(1, channels, width), d_filter


def solution(mesh):
    placed = (
        P("rep", None, "ctx"),
        P("rep", None, "ctx"),
        P("rep", None, "ctx"),
        P("ctx", None),
        P("ctx"),
    )
    grid = (mesh.shape["ctx"] // 8, 4, 2)
    return jax.shard_map(
        functools.partial(on_device, grid),
        mesh=mesh,
        in_specs=placed,
        out_specs=(P("rep", None, "ctx"), P("rep", None, "ctx"), P("ctx", None)),
        check_vma=False,
    )
```
